256 devices in a mesh: tm: 256 (over y, z, x, core).
Axes of the slice: x: 4, y: 4, z: 8, core: 2. Of those that a mesh axis runs over, the one named last changes fastest.
Arguments:
- boundary_inverse: bfloat16 [256, 512, 512], P('tm'), may hold values from -1 to 6, as said below
- coupling: bfloat16 [256, 512, 512], P('tm'), may hold values from -0.15820312 to 0.15820312
- step_inverse: bfloat16 [256, 512, 512], P('tm'), may hold values from -1 to 6, as said below
- step_diagonal: float32 [256, 512], P('tm'), may hold values from 0.5 to 2
- links: bfloat16 [256, 2, 512, 512], P('tm'), may hold values from -0.15820312 to 0.15820312
- arrows: bfloat16 [256, 2, 4, 512], P('tm'), may hold values from -0.30935922 to 0.30935922
- lengths: int32 [256], P('tm'), may hold values from 1 to 2, as said below
Outputs:
- variances: float32 [256, 3, 512], P('tm')
- tip_grad: float32 [4, 4], replicated
The draws below stay inside these ranges and needn't reach their ends.
Inputs may be any that keep to these rules, and one draw needn't show every extreme that they name: `boundary_inverse`: symmetric blocks. `step_inverse`: symmetric blocks. `lengths`: partition 0 has 2 live steps and partition 1 has 1 in every draw.
All inputs are finite; a program needn't handle non-finite values.
Results may differ from the reference program's by a relative error of at most 0.005.
Values may be sent and summed in bfloat16 or wider, within the bound.
No kernel may reach another device: no remote copies, remote signals or barrier semaphores. Data moves between devices by JAX's collectives and lax.ppermute only.
A program may use at most 64 MiB of HBM per device.

```python
import math
import jax
import jax.numpy as jnp
import numpy as np
from jax import lax

B = 512
FIXED = 4
PARTITIONS = 256


def lax_rows(width):
    return jnp.broadcast_to(jnp.arange(width, dtype=jnp.int32)[:, None], (width, width))


def symmetric_blocks(key, scale_spread):
    key_off, key_diag, key_scale = jax.random.split(key, 3)
    noise = jnp.clip(jax.random.normal(key_off, (PARTITIONS, B, B), jnp.float32), -4.0, 4.0)
    offdiag = (noise + jnp.swapaxes(noise, 1, 2)) * (0.7071 * 0.3 / B ** 0.5)
    rows = lax_rows(B)
    columns = jnp.swapaxes(rows, 0, 1)
    gap = jnp.abs(rows - columns).astype(jnp.float32)
    kernel = 0.45 * jnp.exp(-gap * (4.0 / B))
    diag_values = jnp.exp(jax.random.uniform(key_diag, (PARTITIONS, B, 1), jnp.float32, 0.4055, 1.0986))
    eye = (rows == columns).astype(jnp.float32)
    blocks = (offdiag + kernel[None]) * (1.0 - eye)[None] + eye[None] * diag_values
    factors = jnp.exp(jax.random.uniform(key_scale, (PARTITIONS, B, 1), jnp.float32, -scale_spread, scale_spread))
    return blocks * factors * jnp.swapaxes(factors, 1, 2)


def draw_boundary_inverse(key, part):
    key = jax.random.fold_in(key, 11)
    return symmetric_blocks(key, 0.0).astype(jnp.bfloat16)


def draw_step_inverse(key, part):
    key = jax.random.fold_in(key, 23)
    return symmetric_blocks(key, 0.0).astype(jnp.bfloat16)


def draw_arrows(key, part):
    key = jax.random.fold_in(key, 37)
    position = jnp.arange(PARTITIONS, dtype=jnp.float32) / (PARTITIONS - 1.0)
    rise = jnp.sqrt(1.0 + 2.0 * position)[:, None, None, None]
    values = jnp.clip(jax.random.normal(key, (PARTITIONS, 2, FIXED, B), jnp.float32), -4.0, 4.0)
    values = values * rise
    return (values / B ** 0.5).astype(jnp.bfloat16)


def draw_lengths(key, part):
    key = jax.random.fold_in(key, 41)
    values = jax.random.randint(key, (PARTITIONS,), 1, 3, jnp.int32)
    places = jnp.arange(PARTITIONS, dtype=jnp.int32)
    values = jnp.where(places == 0, 2, values)
    return jnp.where(places == 1, 1, values).astype(jnp.int32)


def level_of(stream_key, dims, pieces, low, top_value):
    level, own = 1.0, jax.random.fold_in(stream_key, 6)
    for axis_at, shards_of in pieces:
        draws = jnp.exp(jax.random.uniform(jax.random.fold_in(own, axis_at), (shards_of,), jnp.float32, low / len(pieces), top_value / len(pieces)))
        level = level * jnp.repeat(draws, dims[axis_at] // shards_of).reshape([-1 if axis == axis_at else 1 for axis in range(len(dims))])
    return level


def normal_values(key, dims, scale, limit, cuts=(), held_as=jnp.bfloat16):
    result = scale * jax.random.normal(key, dims, jnp.float32)
    if cuts:
        result = result * level_of(key, dims, cuts, -0.22, 0.18)
    return jnp.clip(result, -limit, limit).astype(held_as)


def setup_inputs(seed: int = 0) -> dict:
    streams_of = jax.random.split(jax.random.key(seed), 8)
    return {
        "boundary_inverse": draw_boundary_inverse(jax.random.fold_in(streams_of[7], 71), 0),
        "coupling": normal_values(streams_of[1], (PARTITIONS, B, B), (0.9 * B ** -0.5), 0.15820312, ((0, 256),)),
        "step_inverse": draw_step_inverse(jax.random.fold_in(streams_of[7], 71), 0),
        "step_diagonal": jnp.clip(jnp.exp(math.log(2.0) - 1.3862944 * jax.random.uniform(streams_of[3], (PARTITIONS, B), jnp.float32) ** level_of(streams_of[3], (PARTITIONS, B), ((0, 256),), -0.2, 0.2)), 0.5, 2.0),
        "links": normal_values(streams_of[4], (PARTITIONS, 2, B, B), (0.9 * B ** -0.5), 0.15820312, ((0, 256),)),
        "arrows": draw_arrows(jax.random.fold_in(streams_of[7], 71), 0),
        "lengths": draw_lengths(jax.random.fold_in(streams_of[7], 71), 0),
    }


def transpose_product(left, right):
    return jnp.dot(left.T, right, preferred_element_type=jnp.float32)


def refresh(inverse, coupler, parent):
    bridge = jnp.dot(parent, coupler, preferred_element_type=jnp.float32).astype(jnp.bfloat16)
    return (inverse.astype(jnp.float32) + transpose_product(coupler, bridge)).astype(jnp.bfloat16)


def arrow_term(arrow, matrix):
    partial_rows = jnp.dot(arrow, matrix, preferred_element_type=jnp.float32)
    return jnp.dot(partial_rows, arrow.astype(jnp.float32).T, precision=lax.Precision.HIGHEST)


def refresh_packed(operands):
    return refresh(operands[0], operands[1], operands[2])


def per_partition(operands):
    boundary, step_inv, extra, link_pair, arrow_pair, length_one = operands
    first_link = link_pair[0]
    second_link = link_pair[1]
    carried = jnp.dot(boundary, first_link, preferred_element_type=jnp.float32).astype(jnp.bfloat16)
    step_state = (step_inv.astype(jnp.float32) + transpose_product(first_link, carried)).astype(jnp.bfloat16)
    final = jnp.dot(step_state, second_link, preferred_element_type=jnp.float32).astype(jnp.bfloat16)
    third = extra + jnp.sum(second_link.astype(jnp.float32) * final.astype(jnp.float32), axis=0)
    third = jnp.where(length_one == 2, third, jnp.zeros_like(third))
    rows = jnp.stack([jnp.diagonal(boundary).astype(jnp.float32), jnp.diagonal(step_state).astype(jnp.float32), third])
    partial_sum = arrow_term(arrow_pair[0], boundary) + arrow_term(arrow_pair[1], step_state)
    return rows, partial_sum


def reference(boundary_inverse, coupling, step_inverse, step_diagonal, links, arrows, lengths):
    levels = PARTITIONS.bit_length() - 1
    states = boundary_inverse
    for height in reversed(range(levels)):
        members = np.arange(1 << height, PARTITIONS, 2 << height).astype(np.int32)
        parents = (members - (1 << height)).astype(np.int32)
        fresh = lax.map(refresh_packed, (boundary_inverse[members], coupling[members], states[parents]))
        states = states.at[members].set(fresh)
    variances, partials = lax.map(per_partition, (states, step_inverse, step_diagonal, links, arrows, lengths))
    return variances, jnp.sum(partials, axis=0) / (2.0 * PARTITIONS)
```

```python
import functools

import jax
import jax.numpy as jnp
from jax import lax
from jax.experimental import pallas as pl
from jax.experimental.pallas import tpu as pltpu
from jax.sharding import PartitionSpec as P

B = 512
T = 128
TILES = B // T
STARTS = [0, 4 * T, 7 * T, 9 * T]
WIDTHS = [4 * T, 3 * T, 2 * T, T]
PACKED = 10 * T
BF = jnp.bfloat16
F32 = jnp.float32

VMEM = pl.BlockSpec(memory_space=pltpu.VMEM)
SMEM = pl.BlockSpec(memory_space=pltpu.SMEM)
ANY = pl.BlockSpec(memory_space=pl.ANY)


def strip(i):
    return slice(STARTS[i], STARTS[i] + WIDTHS[i])


def rows_of(i):
    return slice(i * T, (i + 1) * T)


def mm(a, b):
    return jnp.dot(a, b, preferred_element_type=F32)


def params():
    return pltpu.CompilerParams(vmem_limit_bytes=24 * 2**20)


def cost(products):
    return pl.CostEstimate(
        flops=int(products * 2 * B**3), bytes_accessed=2 * B * B * 2, transcendentals=0
    )


def pack_kernel(full, packed, sems):
    copies = [
        pltpu.make_async_copy(
            full.at[pl.ds(i * T, T), pl.ds(i * T, WIDTHS[i])],
            packed.at[:, pl.ds(STARTS[i], WIDTHS[i])],
            sems.at[i],
        )
        for i in range(TILES)
    ]
    for copy in copies:
        copy.start()
    for copy in copies:
        copy.wait()


def pack(full):
    return pl.pallas_call(
        pack_kernel,
        out_shape=jax.ShapeDtypeStruct((T, PACKED), BF),
        in_specs=[ANY],
        out_specs=VMEM,
        scratch_shapes=[pltpu.SemaphoreType.DMA((TILES,))],
        compiler_params=params(),
        cost_estimate=cost(0.01),
    )(full)


def unpack(packed, full):
    for i in range(TILES):
        row = packed[:, strip(i)]
        full[rows_of(i), i * T :] = row
        for j in range(i + 1, TILES):
            full[rows_of(j), rows_of(i)] = row[:, (j - i) * T : (j - i + 1) * T].T


def level_kernel(active, parent, coupler, coupler_t, state, kept, state_out, kept_out, full, bridge):
    @pl.when(active[0] == 1)
    def _():
        unpack(parent, full)
        bridge[...] = mm(full[...], coupler[...]).astype(BF)
        for i in range(TILES):
            fresh = mm(coupler_t[rows_of(i), :], bridge[:, i * T :])
            state_out[:, strip(i)] = (state[:, strip(i)].astype(F32) + fresh).astype(BF)
        kept_out[...] = parent[...]


def level(active, parent, coupler, coupler_t, state, kept):
    packed = jax.ShapeDtypeStruct((T, PACKED), BF)
    return pl.pallas_call(
        level_kernel,
        out_shape=(packed, packed),
        in_specs=[SMEM] + [VMEM] * 5,
        out_specs=(VMEM, VMEM),
        input_output_aliases={4: 0, 5: 1},
        scratch_shapes=[pltpu.VMEM((B, B), BF), pltpu.VMEM((B, B), BF)],
        compiler_params=params(),
        cost_estimate=cost(2),
    )(active, parent, coupler, coupler_t, state, kept)


def transpose_kernel(a, out):
    out[...] = a[...].T


def transposed(a):
    return pl.pallas_call(
        transpose_kernel,
        out_shape=jax.ShapeDtypeStruct((B, B), BF),
        in_specs=[VMEM],
        out_specs=VMEM,
        compiler_params=params(),
        cost_estimate=cost(1),
    )(a)


def diagonal_row(a, base):
    tile = a[base : base + T, base : base + T]
    rows = lax.broadcasted_iota(jnp.int32, (T, T), 0)
    columns = lax.broadcasted_iota(jnp.int32, (T, T), 1)
    return jnp.sum(jnp.where(rows == columns, tile.astype(F32), 0.0), axis=0, keepdims=True)


def outer_rows(left, right):
    return lax.dot_general(
        left, right, (((1,), (1,)), ((), ())), preferred_element_type=F32,
        precision=lax.Precision.HIGHEST,
    )


def prepare_kernel(
    live, inverse, coupler, coupler_t, step_inverse, step_diagonal, links, arrows,
    factors, constants, rows_out, tip_out, lower, step,
):
    first = links[0, 0]
    second = links[0, 1]
    factors[:, :B] = coupler[...]
    product = mm(coupler[...], first).astype(BF)
    factors[:, B : 2 * B] = product
    factors[:, 2 * B :] = mm(product, second).astype(BF)
    lower[...] = mm(inverse[...], first).astype(BF)
    step[...] = step_inverse[...].astype(F32) + lax.dot_general(
        first, lower[...], (((0,), (0,)), ((), ())), preferred_element_type=F32
    )
    step_b = step[...].astype(BF)
    last = mm(step_b, second)
    extra = jnp.sum(second.astype(F32) * last, axis=0, keepdims=True) + step_diagonal[...]
    for i in range(TILES):
        constants[0:1, rows_of(i)] = diagonal_row(inverse, i * T)
        constants[1:2, rows_of(i)] = diagonal_row(step, i * T)
    constants[2:3, :] = extra
    constants[3:8, :] = jnp.zeros((5, B), F32)
    a0 = arrows[0, 0]
    a1 = arrows[0, 1]
    rows_out[0:4, :] = lax.dot_general(
        a0, coupler[...], (((1,), (1,)), ((), ())), preferred_element_type=F32
    )
    rows_out[4:8, :] = lax.dot_general(
        a1, product, (((1,), (1,)), ((), ())), preferred_element_type=F32
    )
    tip = outer_rows(mm(a0, inverse[...]), a0.astype(F32)) + outer_rows(
        mm(a1, step_b), a1.astype(F32)
    )
    tip_out[...] = jnp.zeros((8, T), F32)
    tip_out[0:4, 0:4] = tip


def prepare(live, inverse, coupler, coupler_t, step_inverse, step_diagonal, links, arrows):
    return pl.pallas_call(
        prepare_kernel,
        out_shape=(
            jax.ShapeDtypeStruct((B, 3 * B), BF),
            jax.ShapeDtypeStruct((8, B), F32),
            jax.ShapeDtypeStruct((8, B), F32),
            jax.ShapeDtypeStruct((8, T), F32),
        ),
        in_specs=[SMEM] + [VMEM] * 7,
        out_specs=(VMEM,) * 4,
        scratch_shapes=[pltpu.VMEM((B, B), BF), pltpu.VMEM((B, B), F32)],
        compiler_params=params(),
        cost_estimate=cost(5),
    )(live, inverse, coupler, coupler_t, step_inverse, step_diagonal, links, arrows)


def tail_kernel(flags, received, kept, factors, constants, rows, tip, variances, tip_out, source):
    leaf = flags[0]

    @pl.when(leaf == 1)
    def _():
        source[...] = received[...]

    @pl.when(leaf != 1)
    def _():
        source[...] = kept[...]

    total = jnp.zeros((1, 3 * B), F32)
    row_b = rows[...].astype(BF)
    partial = []
    for i in range(TILES):
        upper = source[:, strip(i)]
        upper = jnp.concatenate([upper[:, :T] * BF(0.5), upper[:, T:]], axis=1) if i < 3 else upper * BF(0.5)
        product = mm(upper, factors[i * T :, :])
        total = total + jnp.sum(
            product * factors[rows_of(i), :].astype(F32), axis=0, keepdims=True
        )
        spread = mm(row_b[:, rows_of(i)], upper)
        partial.append(spread)
    for i in range(TILES):
        acc = partial[0][:, rows_of(i)]
        for k in range(1, i + 1):
            acc = acc + partial[k][:, (i - k) * T : (i - k + 1) * T]
        partial.append(acc)
    spread = jnp.concatenate(partial[TILES:], axis=1)
    rooted = flags[2] == 1
    total = jnp.where(rooted, 0.0, 2.0 * total)
    both = flags[1] == 2
    variances[0, 0:1, :] = constants[0:1, :] + total[:, :B]
    variances[0, 1:2, :] = constants[1:2, :] + total[:, B : 2 * B]
    variances[0, 2:3, :] = jnp.where(both, constants[2:3, :] + total[:, 2 * B :], 0.0)
    exact = row_b.astype(F32)
    form = outer_rows(spread[0:4], exact[0:4]) + outer_rows(spread[4:8], exact[4:8])
    form = jnp.where(rooted, 0.0, form + form.T)
    tip_out[...] = tip[...]
    tip_out[0:4, 0:4] = tip[0:4, 0:4] + form


def tail(flags, received, kept, factors, constants, rows, tip):
    return pl.pallas_call(
        tail_kernel,
        out_shape=(
            jax.ShapeDtypeStruct((1, 3, B), F32),
            jax.ShapeDtypeStruct((8, T), F32),
        ),
        in_specs=[SMEM] + [VMEM] * 6,
        out_specs=(VMEM, VMEM),
        scratch_shapes=[pltpu.VMEM((T, PACKED), BF)],
        compiler_params=params(),
        cost_estimate=cost(3),
    )(flags, received, kept, factors, constants, rows, tip)


def ring_pairs(devices, height):
    target = {i: i ^ 1 for i in range(devices)}
    if height:
        for child in range(1 << height, devices, 2 << height):
            parent = child - (1 << height)
            target[parent] = child
            target[child] = child + 1
            target[child + 1] = parent + 1
            target[parent + 1] = parent
    return sorted(target.items())


def shards(boundary_inverse, coupling, step_inverse, step_diagonal, links, arrows, lengths):
    blocks = lax.axis_size("tm")
    levels = blocks.bit_length() - 1
    me = lax.axis_index("tm")
    coupler = coupling[0]
    inverse = boundary_inverse[0]
    state = pack(inverse)
    kept = jnp.zeros((T, PACKED), BF)
    coupler_t = transposed(coupler)
    factors, constants, rows, tip = prepare(
        lengths, inverse, coupler, coupler_t, step_inverse[0], step_diagonal, links, arrows
    )
    parent = None
    for height in reversed(range(levels)):
        parent = lax.ppermute(state, "tm", ring_pairs(blocks, height))
        if height:
            active = (me % (2 << height) == 1 << height).astype(jnp.int32)[None]
            state, kept = level(active, parent, coupler, coupler_t, state, kept)
    flags = jnp.stack([me % 2, lengths[0], (me == 0).astype(jnp.int32)]).astype(jnp.int32)
    variances, total = tail(flags, parent, kept, factors, constants, rows, tip)
    for height in range(levels):
        pairs = [(i, i ^ (1 << height)) for i in range(blocks)]
        total = total + lax.ppermute(total, "tm", pairs)
    return variances, total[:4, :4] / (2.0 * blocks)


def solution(mesh):
    in_specs = (
        P("tm", None, None),
        P("tm", None, None),
        P("tm", None, None),
        P("tm", None),
        P("tm", None, None, None),
        P("tm", None, None, None),
        P("tm"),
    )
    out_specs = (P("tm", None, None), P())
    return jax.shard_map(shards, mesh=mesh, in_specs=in_specs, out_specs=out_specs, check_vma=False)
```

```python
import functools

import jax
import jax.numpy as jnp
from jax import lax
from jax.experimental import pallas as pl
from jax.experimental.pallas import tpu as pltpu
from jax.sharding import PartitionSpec as P

B = 512
T = 128
TILES = B // T
STARTS = [0, 4 * T, 7 * T, 9 * T]
WIDTHS = [4 * T, 3 * T, 2 * T, T]
PACKED = 10 * T
BF = jnp.bfloat16
F32 = jnp.float32

VMEM = pl.BlockSpec(memory_space=pltpu.VMEM)
SMEM = pl.BlockSpec(memory_space=pltpu.SMEM)
ANY = pl.BlockSpec(memory_space=pl.ANY)
HBM = pl.BlockSpec(memory_space=pltpu.HBM)


def strip(i):
    return slice(STARTS[i], STARTS[i] + WIDTHS[i])


def rows_of(i):
    return slice(i * T, (i + 1) * T)


def mm(a, b):
    return jnp.dot(a, b, preferred_element_type=F32)


def fetch(sems, *pairs):
    copies = [pltpu.make_async_copy(a, b, sems.at[i]) for i, (a, b) in enumerate(pairs)]
    for copy in copies:
        copy.start()
    for copy in copies:
        copy.wait()


def params():
    return pltpu.CompilerParams(vmem_limit_bytes=12 * 2**20)


def cost(products):
    return pl.CostEstimate(
        flops=int(products * 2 * B**3), bytes_accessed=2 * B * B * 2, transcendentals=0
    )


def open_kernel(full, coupling, packed, coupler, turned, sems):
    load = pltpu.make_async_copy(coupling, coupler, sems.at[TILES])
    load.start()
    copies = [
        pltpu.make_async_copy(
            full.at[pl.ds(i * T, T), pl.ds(i * T, WIDTHS[i])],
            packed.at[:, pl.ds(STARTS[i], WIDTHS[i])],
            sems.at[i],
        )
        for i in range(TILES)
    ]
    for copy in copies:
        copy.start()
    load.wait()
    turned[...] = coupler[...].T
    for copy in copies:
        copy.wait()


def open_blocks(full, coupling):
    block = pltpu.VMEM((B, B), BF)
    return pl.pallas_call(
        open_kernel,
        out_shape=(pltpu.VMEM((T, PACKED), BF), block, block),
        in_specs=[HBM, HBM],
        out_specs=(VMEM,) * 3,
        scratch_shapes=[pltpu.SemaphoreType.DMA((TILES + 1,))],
        compiler_params=params(),
        cost_estimate=cost(0.5),
    )(full, coupling)


def unpack(packed, full):
    for i in range(TILES):
        row = packed[:, strip(i)]
        full[rows_of(i), i * T :] = row
        for j in range(i + 1, TILES):
            full[rows_of(j), rows_of(i)] = row[:, (j - i) * T : (j - i + 1) * T].T


def level_kernel(active, parent, coupler, coupler_t, state, state_out, full, bridge):
    @pl.when(active[0] == 1)
    def _():
        unpack(parent, full)
        bridge[...] = mm(full[...], coupler[...]).astype(BF)
        for i in range(TILES):
            fresh = mm(coupler_t[rows_of(i), :], bridge[:, i * T :])
            state_out[:, strip(i)] = (state[:, strip(i)].astype(F32) + fresh).astype(BF)


def level(active, parent, coupler, coupler_t, state):
    return pl.pallas_call(
        level_kernel,
        out_shape=pltpu.VMEM((T, PACKED), BF),
        in_specs=[SMEM] + [VMEM] * 4,
        out_specs=VMEM,
        input_output_aliases={4: 0},
        scratch_shapes=[pltpu.VMEM((B, B), BF), pltpu.VMEM((B, B), BF)],
        compiler_params=params(),
        cost_estimate=cost(2),
    )(active, parent, coupler, coupler_t, state)


def diagonal_row(a, base):
    tile = a[base : base + T, base : base + T]
    rows = lax.broadcasted_iota(jnp.int32, (T, T), 0)
    columns = lax.broadcasted_iota(jnp.int32, (T, T), 1)
    return jnp.sum(jnp.where(rows == columns, tile.astype(F32), 0.0), axis=0, keepdims=True)


def times_transposed(left, right):
    return lax.dot_general(left, right, (((1,), (1,)), ((), ())), preferred_element_type=F32)


def prepare_kernel(is_leaf, coupler, step_diagonal, inverse_far, step_far, links_far, *refs):
    factors_far, constants, inverse, step_inverse, links, factors, lower, step, sems = refs

    fetch(sems, (inverse_far, inverse), (step_far, step_inverse), (links_far, links))
    first = links[0, 0]
    second = links[0, 1]
    if is_leaf:
        factors[:, :B] = coupler[...]
        factors[:, B : 2 * B] = mm(coupler[...], first).astype(BF)
        lower[...] = mm(inverse[...], first).astype(BF)
        step[...] = step_inverse[...].astype(F32) + lax.dot_general(
            first, lower[...], (((0,), (0,)), ((), ())), preferred_element_type=F32
        )
        for i in range(TILES):
            constants[0:1, rows_of(i)] = diagonal_row(inverse, i * T)
        last = mm(step[...].astype(BF), second)
    else:
        step[...] = step_inverse[...].astype(F32)
        rows = lax.broadcasted_iota(jnp.int32, (B, B), 0)
        columns = lax.broadcasted_iota(jnp.int32, (B, B), 1)
        factors[:, :B] = jnp.where(rows == columns, 1.0, 0.0).astype(BF)
        factors[:, B : 2 * B] = first
        constants[0:1, :] = jnp.zeros((1, B), F32)
        last = mm(step_inverse[...], second)
    factors[:, 2 * B :] = mm(factors[:, B : 2 * B], second).astype(BF)
    extra = jnp.sum(second.astype(F32) * last, axis=0, keepdims=True) + step_diagonal[...]
    for i in range(TILES):
        constants[1:2, rows_of(i)] = diagonal_row(step, i * T)
    constants[2:3, :] = extra
    constants[3:8, :] = jnp.zeros((5, B), F32)
    fetch(sems, (factors, factors_far))


def prepare(is_leaf, coupler, step_diagonal, inverse, step_inverse, links):
    return pl.pallas_call(
        functools.partial(prepare_kernel, is_leaf),
        out_shape=(pltpu.HBM((B, 3 * B), BF), pltpu.VMEM((8, B), F32)),
        in_specs=[VMEM, VMEM, HBM, HBM, HBM],
        out_specs=(HBM, VMEM),
        scratch_shapes=[
            pltpu.VMEM((B, B), BF), pltpu.VMEM((B, B), BF), pltpu.VMEM((1, 2, B, B), BF),
            pltpu.VMEM((B, 3 * B), BF), pltpu.VMEM((B, B), BF), pltpu.VMEM((B, B), F32),
            pltpu.SemaphoreType.DMA((3,)),
        ],
        compiler_params=params(),
        cost_estimate=cost(5),
    )(coupler, step_diagonal, inverse, step_inverse, links)


def load_kernel(far, near, sems):
    fetch(sems, (far, near))


def load(far):
    return pl.pallas_call(
        load_kernel,
        out_shape=pltpu.VMEM(far.shape, far.dtype),
        in_specs=[HBM],
        out_specs=VMEM,
        scratch_shapes=[pltpu.SemaphoreType.DMA((1,))],
        compiler_params=params(),
        cost_estimate=cost(0.5),
    )(pltpu.with_memory_space_constraint(far, pltpu.HBM))


HEAD = 16
GATHERED = 4
ALL_ROWS = 8 << GATHERED


def halved(packed, i):
    row = packed[:, strip(i)]
    diagonal = row[:, :T] * BF(0.5)
    return diagonal if i == TILES - 1 else jnp.concatenate([diagonal, row[:, T:]], axis=1)


def block_forms(left, right):
    count = right.shape[0]
    high = left.astype(BF)
    low = (left - high.astype(F32)).astype(BF)
    gram = times_transposed(high, right) + times_transposed(low, right)
    rows = lax.broadcasted_iota(jnp.int32, (count, count), 0)
    columns = lax.broadcasted_iota(jnp.int32, (count, count), 1)
    gram = jnp.where(rows // 4 == columns // 4, gram, 0.0)
    places = lax.broadcasted_iota(jnp.int32, (count, T), 0)
    lanes = lax.broadcasted_iota(jnp.int32, (count, T), 1)
    chosen = jnp.where(places % 4 == lanes, 1.0, 0.0)
    folded = jnp.dot(gram, chosen, precision=lax.Precision.HIGHEST, preferred_element_type=F32)
    folded = jnp.sum(folded.reshape(count // 8, 8, T), axis=0)
    return jnp.concatenate([folded[:4] + folded[4:], jnp.zeros((4, T), F32)], axis=0)


def packed_forms(rows, packed):
    parts = [mm(rows[:, rows_of(i)], halved(packed, i)) for i in range(TILES)]
    columns = []
    for i in range(TILES):
        column = parts[0][:, rows_of(i)]
        for k in range(1, i + 1):
            column = column + parts[k][:, (i - k) * T : (i - k + 1) * T]
        columns.append(column)
    form = block_forms(jnp.concatenate(columns, axis=1), rows)
    square = jnp.concatenate([form, jnp.zeros((T - 8, T), F32)], axis=0)
    return form + square.T[:8]


def write_constants(message, value):
    high = value.astype(BF).astype(F32)
    head = jnp.concatenate([high, value - high, jnp.zeros((8, T), F32)], axis=0)
    message[0:HEAD, 0:T] = head.astype(BF)


def constants_of(message):
    head = message[0:HEAD, 0:T].astype(F32)
    return jnp.concatenate([head[0:4] + head[4:8], jnp.zeros((4, T), F32)], axis=0)


def own_message_kernel(arrows, links_far, step_far, message, link, step_inverse, sems):
    fetch(sems, (links_far.at[0, 0], link), (step_far, step_inverse))
    a0 = arrows[0, 0]
    a1 = arrows[0, 1]
    through = times_transposed(a1, link[...])
    own = jnp.concatenate([a0.astype(F32), through, jnp.zeros((8, B), F32)], axis=0)
    message[HEAD:, :] = own.astype(BF)
    zeros = jnp.zeros((4, B), BF)
    padded = jnp.concatenate([a1, zeros, zeros, zeros], axis=0)
    write_constants(message, block_forms(mm(padded, step_inverse[...]), padded)[:4])


def own_message(arrows, links, step_inverse):
    return pl.pallas_call(
        own_message_kernel,
        out_shape=jax.ShapeDtypeStruct((HEAD + 16, B), BF),
        in_specs=[VMEM, HBM, HBM],
        out_specs=VMEM,
        scratch_shapes=[
            pltpu.VMEM((B, B), BF), pltpu.VMEM((B, B), BF), pltpu.SemaphoreType.DMA((2,)),
        ],
        compiler_params=params(),
        cost_estimate=cost(0.1),
    )(arrows, links, step_inverse)


def first_eight(message):
    return message[HEAD:, :].astype(F32)[:8]


def chip_rows_kernel(active, own, other, inverse_any, coupler, rows, sums, inverse, sems):
    @pl.when(active[0] == 1)
    def _():
        fetch(sems, (inverse_any, inverse))
        mine = own[HEAD:, :]
        through = times_transposed(mine, coupler[...])
        sums[...] = constants_of(own) + constants_of(other) + block_forms(mm(mine, inverse[...]), mine)
        both = jnp.concatenate([first_eight(other), through[:8]], axis=0)
        rows[0:16, :] = both.astype(BF)


def chip_rows(active, own, other, inverse, coupler):
    return pl.pallas_call(
        chip_rows_kernel,
        out_shape=(pltpu.VMEM((ALL_ROWS, B), BF), pltpu.VMEM((8, T), F32)),
        in_specs=[SMEM, VMEM, VMEM, ANY, VMEM],
        out_specs=(VMEM,) * 2,
        scratch_shapes=[pltpu.VMEM((B, B), BF), pltpu.SemaphoreType.DMA((1,))],
        compiler_params=params(),
        cost_estimate=cost(0.2),
    )(active, own, other, inverse, coupler)


def take_message(stage, message, rows, sums):
    count = 8 << stage
    rows[count : 2 * count, :] = message[HEAD:, :]
    sums[...] = sums[...] + constants_of(message)


def up_kernel(stage, flags, inverse_any, coupler_any, incoming_any, _, __, rows, sums, message, inverse, coupler, incoming, sems):
    if stage > 1:

        @pl.when(flags[0] == 1)
        def _():
            fetch(sems, (incoming_any, incoming))
            take_message(stage - 1, incoming, rows, sums)

    @pl.when(flags[1] == 1)
    def _():
        fetch(sems, (inverse_any, inverse), (coupler_any, coupler))
        own = rows[0 : 8 << stage, :]
        message[HEAD:, :] = times_transposed(own, coupler[...]).astype(BF)
        write_constants(message, (sums[...] + packed_forms(own, inverse))[:4])


def up(stage, flags, inverse, coupler, incoming, rows, sums):
    return pl.pallas_call(
        functools.partial(up_kernel, stage),
        out_shape=(
            pltpu.VMEM((ALL_ROWS, B), BF),
            pltpu.VMEM((8, T), F32),
            pltpu.VMEM((HEAD + (8 << stage), B), BF),
        ),
        in_specs=[SMEM, ANY, ANY, ANY, VMEM, VMEM],
        out_specs=(VMEM,) * 3,
        input_output_aliases={4: 0, 5: 1},
        scratch_shapes=[
            pltpu.VMEM((T, PACKED), BF), pltpu.VMEM((B, B), BF), pltpu.VMEM(incoming.shape, BF),
            pltpu.SemaphoreType.DMA((2,)),
        ],
        compiler_params=params(),
        cost_estimate=cost(0.3),
    )(flags, inverse, coupler, incoming, rows, sums)


def finish_kernel(flags, incoming_any, rows, sums, gathered, incoming, sems):
    @pl.when(flags[0] == 1)
    def _():
        fetch(sems, (incoming_any, incoming))
        half = ALL_ROWS // 2
        gathered[HEAD : HEAD + half, :] = rows[0:half, :]
        gathered[HEAD + half :, :] = incoming[HEAD:, :]
        write_constants(gathered, (sums[...] + constants_of(incoming))[:4])


def finish(flags, incoming, rows, sums):
    return pl.pallas_call(
        finish_kernel,
        out_shape=jax.ShapeDtypeStruct((HEAD + ALL_ROWS, B), BF),
        in_specs=[SMEM, ANY, VMEM, VMEM],
        out_specs=VMEM,
        scratch_shapes=[pltpu.VMEM(incoming.shape, BF), pltpu.SemaphoreType.DMA((1,))],
        compiler_params=params(),
        cost_estimate=cost(0.1),
    )(flags, incoming, rows, sums)


def place_masks():
    rows = lax.broadcasted_iota(jnp.int32, (8, T), 0)
    lanes = lax.broadcasted_iota(jnp.int32, (8, T), 1)
    square_rows = lax.broadcasted_iota(jnp.int32, (T, T), 0)
    square_lanes = lax.broadcasted_iota(jnp.int32, (T, T), 1)
    return lanes // 4 == rows, jnp.where(square_lanes % 4 == square_rows, 1.0, 0.0)


def absorb_kernel(scale, flags, state_any, gathered_any, tip, state, gathered, sems):
    tip[...] = jnp.zeros((1, T), F32)

    @pl.when(flags[0] == 1)
    def _():
        fetch(sems, (state_any, state), (gathered_any, gathered))
        value = constants_of(gathered) + packed_forms(gathered[HEAD:, :], state)
        where, repeat = place_masks()
        spread = jnp.dot(value, repeat, precision=lax.Precision.HIGHEST, preferred_element_type=F32)
        tip[...] = jnp.sum(jnp.where(where, spread, 0.0), axis=0, keepdims=True) * scale


def absorb(scale, flags, state, gathered):
    return pl.pallas_call(
        functools.partial(absorb_kernel, scale),
        out_shape=jax.ShapeDtypeStruct((1, T), F32),
        in_specs=[SMEM, ANY, ANY],
        out_specs=VMEM,
        scratch_shapes=[
            pltpu.VMEM((T, PACKED), BF), pltpu.VMEM(gathered.shape, BF), pltpu.SemaphoreType.DMA((2,)),
        ],
        compiler_params=params(),
        cost_estimate=cost(0.5),
    )(flags, state, gathered)


def tail_kernel(
    flags, received, state, factors, constants, tip, tip_received, variances, tip_out, source
):
    leaf = flags[0]

    @pl.when(leaf == 1)
    def _():
        source[...] = received[...]

    @pl.when(leaf != 1)
    def _():
        source[...] = state[...]

    total = jnp.zeros((1, 3 * B), F32)
    for i in range(TILES):
        product = mm(halved(source, i), factors[i * T :, :])
        total = total + jnp.sum(
            product * factors[rows_of(i), :].astype(F32), axis=0, keepdims=True
        )
    total = 2.0 * total
    variances[0] = constants[0:1, :] + total[:, :B]
    variances[1] = constants[1:2, :] + total[:, B : 2 * B]
    variances[2] = jnp.where(flags[1] == 2, constants[2:3, :] + total[:, 2 * B :], 0.0)
    row = jnp.where(leaf == 1, tip[...], tip_received[...])
    where, repeat = place_masks()
    spread = jnp.where(where, jnp.broadcast_to(row, (8, T)), 0.0)
    square = lax.dot_general(
        spread, repeat, (((1,), (1,)), ((), ())), preferred_element_type=F32,
        precision=lax.Precision.HIGHEST,
    )
    tip_out[...] = square[0:4, 0:4]


def tail(flags, received, state, factors, constants, tip, tip_received):
    return pl.pallas_call(
        tail_kernel,
        out_shape=(
            jax.ShapeDtypeStruct((3, 1, B), F32),
            jax.ShapeDtypeStruct((4, 4), F32),
        ),
        in_specs=[SMEM] + [VMEM] * 6,
        out_specs=(VMEM, VMEM),
        scratch_shapes=[pltpu.VMEM((T, PACKED), BF)],
        compiler_params=params(),
        cost_estimate=cost(3),
    )(flags, received, state, factors, constants, tip, tip_received)


def blank_kernel(out):
    pass


def blank(shape, dtype):
    return pl.pallas_call(
        blank_kernel,
        out_shape=jax.ShapeDtypeStruct(shape, dtype),
        out_specs=ANY,
        compiler_params=params(),
        cost_estimate=cost(0.001),
    )()


def swap_pairs(devices, bit):
    return [(i, i ^ bit) for i in range(devices)]


def chip_cycles(devices, height):
    target = {i: i ^ 1 for i in range(devices)}
    for child in range(1 << height, devices, 2 << height):
        parent = child - (1 << height)
        target[parent] = child
        target[child] = child + 1
        target[child + 1] = parent + 1
        target[parent + 1] = parent
    return sorted(target.items())


def neighbour_cycles(devices, height):
    target = {i: i ^ 1 for i in range(devices)}
    for child in range(1 << height, devices, 2 << height):
        for core in range(2):
            first, second = child - (1 << height) + core, child + core
            target[first] = second
            target[second] = second + 2
            target[second + 2] = first + 2
            target[first + 2] = first
    return sorted(target.items())


def children(devices, height):
    return [(i, i + (1 << height)) for i in range(0, devices, 2 << height)]


def after(arrays, *others):
    return lax.optimization_barrier((arrays, others))[0]


def integers(*values):
    return jnp.stack([jnp.asarray(value, jnp.int32) for value in values])


def shards(boundary_inverse, coupling, step_inverse, step_diagonal, links, arrows, lengths):
    blocks = lax.axis_size("tm")
    me = lax.axis_index("tm")
    chip = me - me % 2
    on_core_one = me % 2 == 1
    inverse = boundary_inverse[0]
    step_inv = step_inverse[0]
    swap = swap_pairs(blocks, 1)
    absorbs = chip % (1 << GATHERED) == 0

    def send(array, pairs):
        return lax.ppermute(array, "tm", pairs)

    def descend(height, parent, state):
        active = integers(me % (2 << height) == 1 << height)
        return level(active, parent, coupler, turned, state)

    def takes_part(height):
        return me % (1 << height) <= 2

    def is_sender(stage):
        return chip % (2 << stage) == 1 << stage

    def is_receiver(stage):
        return chip % (2 << stage) == 0

    state, coupler, turned = open_blocks(inverse, coupling[0])

    parent = send(state, chip_cycles(blocks, 7))
    given = after((arrows, links, step_inv), state)
    mine = own_message(*given)
    coupler_zero = send(coupler, swap)
    message_zero = send(mine, swap)
    block_zero = parent
    parent, coupler_zero, message_zero = lax.optimization_barrier((parent, coupler_zero, message_zero))
    state = descend(7, parent, state)

    def tree_top(state):
        for height in (6, 5):
            state = lax.cond(
                takes_part(height),
                lambda s, h=height: descend(h, send(s, neighbour_cycles(blocks, h)), s),
                lambda s: s,
                state,
            )

        def ready(state):
            given = after((step_diagonal, inverse, step_inv, links), state)
            return prepare(False, coupler, *given)

        def last(state):
            parent = send(state, neighbour_cycles(blocks, 4))
            prepared = ready(state)
            parent, prepared = lax.optimization_barrier((parent, prepared))
            return [descend(4, parent, state), *prepared]

        state, factors, constants = lax.cond(
            takes_part(4), last, lambda s: [s, *ready(s)], state
        )
        return [state, blank((HEAD + ALL_ROWS, B), BF), factors, constants]

    def gather_rows(state):
        rows, sums = chip_rows(integers(1), mine, message_zero, inverse, coupler)
        message = message_zero
        for stage in (1, 2, 3):
            flags = integers(is_receiver(stage - 1), is_sender(stage))
            rows, sums, message = up(stage, flags, block_zero, coupler_zero, message, rows, sums)
            message = send(message, swap_pairs(blocks, 1 << stage))
        gathered = finish(integers(absorbs), message, rows, sums)
        given = after((step_diagonal, inverse, step_inv, links), gathered)
        return [state, gathered, *prepare(True, coupler, *given)]

    state, gathered, factors, constants = lax.cond(on_core_one, gather_rows, tree_top, state)
    state_zero = lax.cond(
        absorbs, lambda s: send(s, swap), lambda s: blank((T, PACKED), BF), state
    )

    def sum_tips(state):
        tip = absorb(1.0 / (2 * blocks), integers(absorbs), state_zero, gathered)
        every = lax.all_to_all(
            jnp.broadcast_to(tip[None], (blocks // 2, 1, T)), "tm", 0, 0,
            axis_index_groups=[list(range(core, blocks, 2)) for core in range(2)],
        )
        return [state, jnp.sum(every, axis=0)]

    def tree_bottom(state):
        state = lax.cond(
            takes_part(3), lambda s: descend(3, send(s, neighbour_cycles(blocks, 3)), s), lambda s: s, state
        )
        for height in (2, 1):
            state = descend(height, send(state, children(blocks, height)), state)
        return [state, blank((1, T), F32)]

    state, tip = lax.cond(on_core_one, sum_tips, tree_bottom, state)
    parent = send(state, swap)
    tip_received = send(tip, swap)
    flags = integers(me % 2, lengths[0])
    near = load(after(factors, state))
    parent, near = lax.optimization_barrier((parent, near))
    variances, total = tail(flags, parent, state, near, constants, tip, tip_received)
    return jnp.transpose(variances, (1, 0, 2)), total


def solution(mesh):
    in_specs = (
        P("tm", None, None),
        P("tm", None, None),
        P("tm", None, None),
        P("tm", None),
        P("tm", None, None, None),
        P("tm", None, None, None),
        P("tm"),
    )
    out_specs = (P("tm", None, None), P())
    return jax.shard_map(shards, mesh=mesh, in_specs=in_specs, out_specs=out_specs, check_vma=False)
```

```python
import functools

import jax
import jax.numpy as jnp
from jax import lax
from jax.experimental import pallas as pl
from jax.experimental.pallas import tpu as pltpu
from jax.sharding import PartitionSpec as P

B = 512
T = 128
TILES = B // T
STARTS = [0, 4 * T, 7 * T, 9 * T]
WIDTHS = [4 * T, 3 * T, 2 * T, T]
PACKED = 10 * T
BF = jnp.bfloat16
F32 = jnp.float32

VMEM = pl.BlockSpec(memory_space=pltpu.VMEM)
SMEM = pl.BlockSpec(memory_space=pltpu.SMEM)
ANY = pl.BlockSpec(memory_space=pl.ANY)
HBM = pl.BlockSpec(memory_space=pltpu.HBM)


def strip(i):
    return slice(STARTS[i], STARTS[i] + WIDTHS[i])


def rows_of(i):
    return slice(i * T, (i + 1) * T)


def mm(a, b):
    return jnp.dot(a, b, preferred_element_type=F32)


def fetch(sems, *pairs):
    copies = [pltpu.make_async_copy(a, b, sems.at[i]) for i, (a, b) in enumerate(pairs)]
    for copy in copies:
        copy.start()
    for copy in copies:
        copy.wait()


def params():
    return pltpu.CompilerParams(vmem_limit_bytes=12 * 2**20)


def cost(products):
    return pl.CostEstimate(
        flops=int(products * 2 * B**3), bytes_accessed=int(min(products, 1) * 4 * B * B), transcendentals=0
    )


def pack_kernel(full, packed, sems):
    fetch(
        sems,
        *[
            (full.at[pl.ds(i * T, T), pl.ds(i * T, WIDTHS[i])], packed.at[:, pl.ds(STARTS[i], WIDTHS[i])])
            for i in range(TILES)
        ],
    )


def pack(full):
    return pl.pallas_call(
        pack_kernel,
        out_shape=pltpu.VMEM((T, PACKED), BF),
        in_specs=[HBM],
        out_specs=VMEM,
        scratch_shapes=[pltpu.SemaphoreType.DMA((TILES,))],
        compiler_params=params(),
        cost_estimate=cost(0.01),
    )(pltpu.with_memory_space_constraint(full, pltpu.HBM))


def open_kernel(coupling, coupler, turned, sems):
    fetch(sems, (coupling, coupler))
    turned[...] = coupler[...].T


def open_coupler(coupling):
    block = pltpu.VMEM((B, B), BF)
    return pl.pallas_call(
        open_kernel,
        out_shape=(block, block),
        in_specs=[HBM],
        out_specs=(VMEM,) * 2,
        scratch_shapes=[pltpu.SemaphoreType.DMA((1,))],
        compiler_params=params(),
        cost_estimate=cost(0.001),
    )(pltpu.with_memory_space_constraint(coupling, pltpu.HBM))


def copy_kernel(a, out):
    out[...] = a[...]


def copied(a):
    return pl.pallas_call(
        copy_kernel,
        out_shape=pltpu.VMEM(a.shape, a.dtype),
        in_specs=[VMEM],
        out_specs=VMEM,
        compiler_params=params(),
        cost_estimate=cost(0.5),
    )(a)


def unpack(packed, full):
    for i in range(TILES):
        row = packed[:, strip(i)]
        full[rows_of(i), i * T :] = row
        for j in range(i + 1, TILES):
            full[rows_of(j), rows_of(i)] = row[:, (j - i) * T : (j - i + 1) * T].T


def level_kernel(active, parent, coupler, coupler_t, state, state_out, full, bridge):
    @pl.when(active[0] == 1)
    def _():
        unpack(parent, full)
        bridge[...] = mm(full[...], coupler[...]).astype(BF)
        for i in range(TILES):
            fresh = mm(coupler_t[rows_of(i), :], bridge[:, i * T :])
            state_out[:, strip(i)] = (state[:, strip(i)].astype(F32) + fresh).astype(BF)


def level(active, parent, coupler, coupler_t, state):
    return pl.pallas_call(
        level_kernel,
        out_shape=pltpu.VMEM((T, PACKED), BF),
        in_specs=[SMEM] + [VMEM] * 4,
        out_specs=VMEM,
        input_output_aliases={4: 0},
        scratch_shapes=[pltpu.VMEM((B, B), BF), pltpu.VMEM((B, B), BF)],
        compiler_params=params(),
        cost_estimate=cost(2),
    )(active, parent, coupler, coupler_t, state)


def diagonal_row(a, top, left):
    tile = a[top : top + T, left : left + T]
    rows = lax.broadcasted_iota(jnp.int32, (T, T), 0)
    columns = lax.broadcasted_iota(jnp.int32, (T, T), 1)
    return jnp.sum(jnp.where(rows == columns, tile.astype(F32), 0.0), axis=0, keepdims=True)


def times_transposed(left, right):
    return lax.dot_general(left, right, (((1,), (1,)), ((), ())), preferred_element_type=F32)


def prepare_kernel(
    is_leaf, active, coupler, step_diagonal, inverse_far, step_far, links_far, _, __, factors, constants,
    inverse, step_inverse, first, second, lower, step, sems,
):
    @pl.when(active[0] == 1)
    def _():
        loads = [
            pltpu.make_async_copy(far, near, sems.at[i])
            for i, (far, near) in enumerate(
                [(links_far.at[0, 0], first), (inverse_far, inverse), (step_far, step_inverse), (links_far.at[0, 1], second)]
            )
        ]
        for copy in loads:
            copy.start()
        loads[0].wait()
        if is_leaf:
            factors[:, :B] = mm(coupler[...], first[...]).astype(BF)
        else:
            factors[:, :B] = first[...]
        loads[1].wait()
        if is_leaf:
            lower[...] = mm(inverse[...], first[...]).astype(BF)
            for i in range(TILES):
                constants[0:1, rows_of(i)] = diagonal_row(inverse, i * T, i * T)
        else:
            constants[0:1, :] = jnp.zeros((1, B), F32)
        loads[2].wait()
        if is_leaf:
            step[...] = step_inverse[...].astype(F32) + lax.dot_general(
                first[...], lower[...], (((0,), (0,)), ((), ())), preferred_element_type=F32
            )
        else:
            step[...] = step_inverse[...].astype(F32)
        for i in range(TILES):
            constants[1:2, rows_of(i)] = diagonal_row(step, i * T, i * T)
        loads[3].wait()
        factors[:, B:] = mm(factors[:, :B], second[...]).astype(BF)
        last = mm(step[...].astype(BF), second[...])
        extra = jnp.sum(second[...].astype(F32) * last, axis=0, keepdims=True) + step_diagonal[...]
        constants[2:3, :] = extra
        constants[3:8, :] = jnp.zeros((5, B), F32)


def prepare(is_leaf, active, coupler, step_diagonal, inverse, step_inverse, links, factors, constants):
    far = [pltpu.with_memory_space_constraint(a, pltpu.HBM) for a in (inverse, step_inverse, links)]
    block = pltpu.VMEM((B, B), BF)
    return pl.pallas_call(
        functools.partial(prepare_kernel, is_leaf),
        out_shape=(pltpu.VMEM((B, 2 * B), BF), pltpu.VMEM((8, B), F32)),
        in_specs=[SMEM, VMEM, VMEM, HBM, HBM, HBM, VMEM, VMEM],
        out_specs=(VMEM, VMEM),
        input_output_aliases={6: 0, 7: 1},
        scratch_shapes=[block, block, block, block, block, pltpu.VMEM((B, B), F32), pltpu.SemaphoreType.DMA((4,))],
        compiler_params=params(),
        cost_estimate=cost(5),
    )(active, coupler, step_diagonal, *far, factors, constants)


HEAD = 16
GATHERED = 4
ALL_ROWS = 8 << GATHERED


def halved(packed, i):
    row = packed[:, strip(i)]
    diagonal = row[:, :T] * BF(0.5)
    return diagonal if i == TILES - 1 else jnp.concatenate([diagonal, row[:, T:]], axis=1)


def block_forms(left, right):
    count = right.shape[0]
    high = left.astype(BF)
    low = (left - high.astype(F32)).astype(BF)
    gram = times_transposed(high, right) + times_transposed(low, right)
    rows = lax.broadcasted_iota(jnp.int32, (count, count), 0)
    columns = lax.broadcasted_iota(jnp.int32, (count, count), 1)
    gram = jnp.where(rows // 4 == columns // 4, gram, 0.0)
    folded = jnp.sum(gram.reshape(count // 8, 8, count), axis=0)
    folded = jnp.concatenate([folded[:4] + folded[4:], jnp.zeros((4, count), F32)], axis=0)
    if count < T:
        folded = jnp.concatenate([folded, jnp.zeros((8, T - count), F32)], axis=1)
    shift = T // 2
    while shift >= 4:
        folded = folded + pltpu.roll(folded, shift, 1)
        shift //= 2
    lanes = lax.broadcasted_iota(jnp.int32, (8, T), 1)
    return jnp.where(lanes < 4, folded, 0.0)


def packed_forms(rows, packed):
    parts = [mm(rows[:, rows_of(i)], halved(packed, i)) for i in range(TILES)]
    columns = []
    for i in range(TILES):
        column = parts[0][:, rows_of(i)]
        for k in range(1, i + 1):
            column = column + parts[k][:, (i - k) * T : (i - k + 1) * T]
        columns.append(column)
    form = block_forms(jnp.concatenate(columns, axis=1), rows)
    square = jnp.concatenate([form, jnp.zeros((T - 8, T), F32)], axis=0)
    return form + square.T[:8]


def write_constants(message, value):
    high = value.astype(BF).astype(F32)
    head = jnp.concatenate([high, value - high, jnp.zeros((8, T), F32)], axis=0)
    message[0:HEAD, 0:T] = head.astype(BF)


def constants_of(message):
    head = message[0:HEAD, 0:T].astype(F32)
    return jnp.concatenate([head[0:4] + head[4:8], jnp.zeros((4, T), F32)], axis=0)


def own_message_kernel(arrows, links_far, step_far, message, link, step_inverse, sems):
    fetch(sems, (links_far.at[0, 0], link), (step_far, step_inverse))
    a0 = arrows[0, 0]
    a1 = arrows[0, 1]
    through = times_transposed(a1, link[...])
    own = jnp.concatenate([a0.astype(F32), through, jnp.zeros((8, B), F32)], axis=0)
    message[HEAD:, :] = own.astype(BF)
    zeros = jnp.zeros((4, B), BF)
    padded = jnp.concatenate([a1, zeros, zeros, zeros], axis=0)
    write_constants(message, block_forms(mm(padded, step_inverse[...]), padded)[:4])


def own_message(arrows, links, step_inverse):
    return pl.pallas_call(
        own_message_kernel,
        out_shape=jax.ShapeDtypeStruct((HEAD + 16, B), BF),
        in_specs=[VMEM, HBM, HBM],
        out_specs=VMEM,
        scratch_shapes=[
            pltpu.VMEM((B, B), BF), pltpu.VMEM((B, B), BF), pltpu.SemaphoreType.DMA((2,)),
        ],
        compiler_params=params(),
        cost_estimate=cost(0.001),
    )(arrows, *[pltpu.with_memory_space_constraint(a, pltpu.HBM) for a in (links, step_inverse)])


def first_eight(message):
    return message[HEAD:, :].astype(F32)[:8]


HALF = ALL_ROWS // 2


def chip_rows_kernel(own, other, coupler, rows):
    rows[...] = jnp.zeros((HALF, B), BF)
    through = times_transposed(own[HEAD:, :], coupler[...])
    rows[0:16, :] = jnp.concatenate([first_eight(other), through[:8]], axis=0).astype(BF)


def chip_rows(own, other, coupler):
    return pl.pallas_call(
        chip_rows_kernel,
        out_shape=pltpu.VMEM((HALF, B), BF),
        in_specs=[VMEM] * 3,
        out_specs=VMEM,
        compiler_params=params(),
        cost_estimate=cost(0.2),
    )(own, other, coupler)


def chip_constants_kernel(own, other, inverse_far, sums, inverse, sems):
    fetch(sems, (inverse_far, inverse))
    mine = own[HEAD:, :]
    sums[...] = constants_of(own) + constants_of(other) + block_forms(mm(mine, inverse[...]), mine)


def chip_constants(own, other, inverse):
    return pl.pallas_call(
        chip_constants_kernel,
        out_shape=jax.ShapeDtypeStruct((8, T), F32),
        in_specs=[VMEM, VMEM, HBM],
        out_specs=VMEM,
        scratch_shapes=[pltpu.VMEM((B, B), BF), pltpu.SemaphoreType.DMA((1,))],
        compiler_params=params(),
        cost_estimate=cost(0.2),
    )(own, other, pltpu.with_memory_space_constraint(inverse, pltpu.HBM))


def up_kernel(stage, flags, coupler_any, incoming_any, _, rows, message, coupler, sems):
    if stage > 1:

        @pl.when(flags[0] == 1)
        def _():
            count = 8 << (stage - 1)
            fetch(sems, (incoming_any, rows.at[pl.ds(count, count)]))

    @pl.when(flags[1] == 1)
    def _():
        fetch(sems, (coupler_any, coupler))
        message[...] = times_transposed(rows[0 : 8 << stage, :], coupler[...]).astype(BF)


def up(stage, flags, coupler, incoming, rows):
    return pl.pallas_call(
        functools.partial(up_kernel, stage),
        out_shape=(pltpu.VMEM((HALF, B), BF), pltpu.VMEM((8 << stage, B), BF)),
        in_specs=[SMEM, ANY, ANY, VMEM],
        out_specs=(VMEM,) * 2,
        input_output_aliases={3: 0},
        scratch_shapes=[pltpu.VMEM((B, B), BF), pltpu.SemaphoreType.DMA((1,))],
        compiler_params=params(),
        cost_estimate=cost(0.3),
    )(flags, coupler, incoming, rows)


def finish_kernel(rows, out):
    out[...] = rows[...]


def finish(rows):
    return pl.pallas_call(
        finish_kernel,
        out_shape=jax.ShapeDtypeStruct(rows.shape, BF),
        in_specs=[VMEM],
        out_specs=VMEM,
        compiler_params=params(),
        cost_estimate=cost(0.1),
    )(rows)


def absorb_kernel(
    scale, flags, block_any, state_any, incoming_any, rows, sums, tip, block, incoming, sems
):
    def add_to_row(value):
        row = value[0:1]
        for j in range(1, 4):
            row = row + pltpu.roll(value[j : j + 1], 4 * j, 1)
        tip[...] = row * scale

    @pl.when(flags[0] == 1)
    def _():
        fetch(sems, (state_any, block), (incoming_any, incoming))
        add_to_row(sums[...] + packed_forms(rows[...], block) + packed_forms(incoming[...], block))

    @pl.when(flags[0] != 1)
    def _():
        fetch(sems, (block_any, block))
        add_to_row(sums[...] + packed_forms(rows[...], block))


def absorb(scale, flags, block_zero, state_zero, incoming, rows, sums):
    return pl.pallas_call(
        functools.partial(absorb_kernel, scale),
        out_shape=jax.ShapeDtypeStruct((1, T), F32),
        in_specs=[SMEM, ANY, ANY, ANY, VMEM, VMEM],
        out_specs=VMEM,
        scratch_shapes=[
            pltpu.VMEM((T, PACKED), BF), pltpu.VMEM(incoming.shape, BF), pltpu.SemaphoreType.DMA((2,)),
        ],
        compiler_params=params(),
        cost_estimate=cost(0.5),
    )(flags, block_zero, state_zero, incoming, rows, sums)


def tail_kernel(
    flags, received, state, coupler, factors, constants, tip, tip_received, variances, tip_out, source
):
    leaf = flags[0]

    @pl.when(leaf == 1)
    def _():
        source[...] = received[...]
        own = jnp.zeros((1, B), F32)
        for i in range(TILES):
            product = mm(halved(source, i), coupler[i * T :, :])
            own = own + jnp.sum(product * coupler[rows_of(i), :].astype(F32), axis=0, keepdims=True)
        variances[0] = constants[0:1, :] + 2.0 * own

    @pl.when(leaf != 1)
    def _():
        source[...] = state[...]
        for i in range(TILES):
            variances[0, :, rows_of(i)] = diagonal_row(state, 0, STARTS[i])

    total = jnp.zeros((1, 2 * B), F32)
    for i in range(TILES):
        product = mm(halved(source, i), factors[i * T :, :])
        total = total + jnp.sum(
            product * factors[rows_of(i), :].astype(F32), axis=0, keepdims=True
        )
    total = 2.0 * total
    variances[1] = constants[1:2, :] + total[:, :B]
    variances[2] = jnp.where(flags[1] == 2, constants[2:3, :] + total[:, B:], 0.0)
    row = jnp.where(leaf == 1, tip[...], tip_received[...])
    for j in range(4):
        turned = row if j == 0 else pltpu.roll(row, T - 4 * j, 1)
        tip_out[j : j + 1, :] = turned[:, 0:4]


def tail(flags, received, state, coupler, factors, constants, tip, tip_received):
    return pl.pallas_call(
        tail_kernel,
        out_shape=(
            jax.ShapeDtypeStruct((3, 1, B), F32),
            jax.ShapeDtypeStruct((4, 4), F32),
        ),
        in_specs=[SMEM] + [VMEM] * 7,
        out_specs=(VMEM, VMEM),
        scratch_shapes=[pltpu.VMEM((T, PACKED), BF)],
        compiler_params=params(),
        cost_estimate=cost(3),
    )(flags, received, state, coupler, factors, constants, tip, tip_received)


def blank_kernel(out):
    pass


def blank(shape, dtype, kind=jax.ShapeDtypeStruct):
    return pl.pallas_call(
        blank_kernel,
        out_shape=kind(shape, dtype),
        out_specs=VMEM if kind is pltpu.VMEM else ANY,
        compiler_params=params(),
        cost_estimate=cost(0.001),
    )()


def swap_pairs(devices, bit):
    return [(i, i ^ bit) for i in range(devices)]


def chip_cycles(devices, height):
    target = {i: i ^ 1 for i in range(devices)}
    for child in range(1 << height, devices, 2 << height):
        parent = child - (1 << height)
        target[parent] = child
        target[child] = child + 1
        target[child + 1] = parent + 1
        target[parent + 1] = parent
    return sorted(target.items())


def neighbour_cycles(devices, height, offset):
    target = {i: i ^ 1 for i in range(devices)}
    for child in range(1 << height, devices, 2 << height):
        for core in range(2):
            first, second = child - (1 << height) + core, child + core
            target[first] = second
            target[second] = second + offset
            target[second + offset] = first + offset
            target[first + offset] = first
    return sorted(target.items())


def children(devices, height):
    return [(i, i + (1 << height)) for i in range(0, devices, 2 << height)]


def after(arrays, *others):
    return lax.optimization_barrier((arrays, others))[0]


def integers(*values):
    return jnp.stack([jnp.asarray(value, jnp.int32) for value in values])


def shards(boundary_inverse, coupling, step_inverse, step_diagonal, links, arrows, lengths):
    blocks = lax.axis_size("tm")
    me = lax.axis_index("tm")
    chip = me - me % 2
    on_core_one = me % 2 == 1
    inverse = boundary_inverse[0]
    step_inv = step_inverse[0]
    swap = swap_pairs(blocks, 1)
    absorbs = chip % (1 << GATHERED) == 0

    def send(array, pairs):
        return lax.ppermute(array, "tm", pairs)

    def descend(height, parent, state):
        active = integers(me % (2 << height) == 1 << height)
        return level(active, parent, coupler, turned, state)

    def helper(height):
        return 6 if height % 2 else 2

    def takes_part(height):
        place = me % (1 << height)
        return (place == 0) | (place == helper(height))

    def is_sender(stage):
        return chip % (2 << stage) == 1 << stage

    def is_receiver(stage):
        return chip % (2 << stage) == 0

    state = pack(inverse)

    parent = send(state, chip_cycles(blocks, 7))
    given = after((arrows, links, step_inv), state)
    mine = own_message(*given)
    factors = blank((B, 2 * B), BF, pltpu.VMEM)
    constants = blank((8, B), F32, pltpu.VMEM)
    coupler, turned = open_coupler(after(coupling[0], mine))
    coupler_zero = send(coupling[0], swap)
    message_zero = send(mine, swap)
    block_zero = parent
    parent, coupler_zero, message_zero = lax.optimization_barrier((parent, coupler_zero, message_zero))
    state = descend(7, parent, state)

    def get_ready(is_leaf, active, factors, constants, *others):
        given = after((step_diagonal, inverse, step_inv, links), *others)
        return list(prepare(is_leaf, integers(active), coupler, *given, factors, constants))

    def tree_top(state, factors, constants):
        factors, constants = get_ready(False, chip % 64 != 0, factors, constants)
        for height in (6, 5, 4):
            state = lax.cond(
                takes_part(height),
                lambda s, h=height: descend(h, send(s, neighbour_cycles(blocks, h, helper(h))), s),
                lambda s: s,
                state,
            )
        return [state, blank((HALF, B), BF), blank((HALF, B), BF), blank((8, T), F32), factors, constants]

    def gather_rows(state, factors, constants):
        rows = chip_rows(mine, message_zero, coupler)
        message = message_zero
        sums = None
        for stage in range(1, GATHERED):
            flags = integers(is_receiver(stage - 1), is_sender(stage))
            rows, message = up(stage, flags, coupler_zero, message, rows)
            message = send(message, swap_pairs(blocks, 1 << stage))
            if sums is None:
                sums = chip_constants(mine, message_zero, after(inverse, rows))
                message, sums = lax.optimization_barrier((message, sums))
        rows = finish(rows)
        return [state, rows, message, sums, *get_ready(True, 1, factors, constants, message)]

    state, rows, message, sums, factors, constants = lax.cond(
        on_core_one, gather_rows, tree_top, state, factors, constants
    )

    def middle(state, factors, constants):
        parent = send(copied(state), chip_cycles(blocks, 3))
        state_zero = send(state, swap)
        factors, constants = get_ready(False, me % 64 == 0, factors, constants, state)
        parent, state_zero, factors, constants = lax.optimization_barrier(
            (parent, state_zero, factors, constants)
        )
        return [descend(3, parent, state), state_zero, factors, constants]

    state, state_zero, factors, constants = lax.cond(
        chip % 8 == 0, middle, lambda s, f, c: [s, blank((T, PACKED), BF), f, c], state, factors, constants
    )

    def sum_tips(state):
        tip = absorb(1.0 / (2 * blocks), integers(absorbs), block_zero, state_zero, message, rows, sums)
        every = lax.all_to_all(
            jnp.broadcast_to(tip[None], (blocks // 2, 1, T)), "tm", 0, 0,
            axis_index_groups=[list(range(core, blocks, 2)) for core in range(2)],
        )
        return [state, jnp.sum(every, axis=0)]

    def tree_bottom(state):
        for height in (2, 1):
            state = descend(height, send(state, children(blocks, height)), state)
        return [state, blank((1, T), F32)]

    state, tip = lax.cond(on_core_one, sum_tips, tree_bottom, state)
    parent = send(state, swap)
    tip_received = send(tip, swap)
    flags = integers(me % 2, lengths[0])
    variances, total = tail(flags, parent, state, coupler, factors, constants, tip, tip_received)
    return jnp.transpose(variances, (1, 0, 2)), total


def solution(mesh):
    in_specs = (
        P("tm", None, None),
        P("tm", None, None),
        P("tm", None, None),
        P("tm", None),
        P("tm", None, None, None),
        P("tm", None, None, None),
        P("tm"),
    )
    out_specs = (P("tm", None, None), P())
    return jax.shard_map(shards, mesh=mesh, in_specs=in_specs, out_specs=out_specs, check_vma=False)
```

```python
import functools

import jax
import jax.numpy as jnp
from jax import lax
from jax.experimental import pallas as pl
from jax.experimental.pallas import tpu as pltpu
from jax.sharding import PartitionSpec as P

B = 512
T = 128
TILES = B // T
STARTS = [0, 4 * T, 7 * T, 9 * T]
WIDTHS = [4 * T, 3 * T, 2 * T, T]
PACKED = 10 * T
BF = jnp.bfloat16
F32 = jnp.float32

VMEM = pl.BlockSpec(memory_space=pltpu.VMEM)
SMEM = pl.BlockSpec(memory_space=pltpu.SMEM)
ANY = pl.BlockSpec(memory_space=pl.ANY)
HBM = pl.BlockSpec(memory_space=pltpu.HBM)


def strip(i):
    return slice(STARTS[i], STARTS[i] + WIDTHS[i])


def rows_of(i):
    return slice(i * T, (i + 1) * T)


def mm(a, b):
    return jnp.dot(a, b, preferred_element_type=F32)


def fetch(sems, *pairs):
    copies = [pltpu.make_async_copy(a, b, sems.at[i]) for i, (a, b) in enumerate(pairs)]
    for copy in copies:
        copy.start()
    for copy in copies:
        copy.wait()


def params():
    return pltpu.CompilerParams(vmem_limit_bytes=12 * 2**20)


def cost(products):
    return pl.CostEstimate(
        flops=int(products * 2 * B**3), bytes_accessed=int(min(products, 1) * 4 * B * B), transcendentals=0
    )


def pack_kernel(full, packed, sems):
    fetch(
        sems,
        *[
            (full.at[pl.ds(i * T, T), pl.ds(i * T, WIDTHS[i])], packed.at[:, pl.ds(STARTS[i], WIDTHS[i])])
            for i in range(TILES)
        ],
    )


def pack(full):
    return pl.pallas_call(
        pack_kernel,
        out_shape=pltpu.VMEM((T, PACKED), BF),
        in_specs=[HBM],
        out_specs=VMEM,
        scratch_shapes=[pltpu.SemaphoreType.DMA((TILES,))],
        compiler_params=params(),
        cost_estimate=cost(0.01),
    )(pltpu.with_memory_space_constraint(full, pltpu.HBM))


def open_kernel(coupling, coupler, turned, sems):
    fetch(sems, (coupling, coupler))
    turned[...] = coupler[...].T


def open_coupler(coupling):
    block = pltpu.VMEM((B, B), BF)
    return pl.pallas_call(
        open_kernel,
        out_shape=(block, block),
        in_specs=[HBM],
        out_specs=(VMEM,) * 2,
        scratch_shapes=[pltpu.SemaphoreType.DMA((1,))],
        compiler_params=params(),
        cost_estimate=cost(0.001),
    )(pltpu.with_memory_space_constraint(coupling, pltpu.HBM))


def copy_kernel(a, out):
    out[...] = a[...]


def copied(a):
    return pl.pallas_call(
        copy_kernel,
        out_shape=pltpu.VMEM(a.shape, a.dtype),
        in_specs=[VMEM],
        out_specs=VMEM,
        compiler_params=params(),
        cost_estimate=cost(0.5),
    )(a)


def unpack(packed, full):
    for i in range(TILES):
        row = packed[:, strip(i)]
        full[rows_of(i), i * T :] = row
        for j in range(i + 1, TILES):
            full[rows_of(j), rows_of(i)] = row[:, (j - i) * T : (j - i + 1) * T].T


def level_kernel(active, parent, coupler, coupler_t, state, state_out, full, bridge):
    @pl.when(active[0] == 1)
    def _():
        unpack(parent, full)
        bridge[...] = mm(full[...], coupler[...]).astype(BF)
        for i in range(TILES):
            fresh = mm(coupler_t[rows_of(i), :], bridge[:, i * T :])
            state_out[:, strip(i)] = (state[:, strip(i)].astype(F32) + fresh).astype(BF)


def level(active, parent, coupler, coupler_t, state):
    return pl.pallas_call(
        level_kernel,
        out_shape=pltpu.VMEM((T, PACKED), BF),
        in_specs=[SMEM] + [VMEM] * 4,
        out_specs=VMEM,
        input_output_aliases={4: 0},
        scratch_shapes=[pltpu.VMEM((B, B), BF), pltpu.VMEM((B, B), BF)],
        compiler_params=params(),
        cost_estimate=cost(2),
    )(active, parent, coupler, coupler_t, state)


def diagonal_row(a, top, left):
    tile = a[top : top + T, left : left + T]
    rows = lax.broadcasted_iota(jnp.int32, (T, T), 0)
    columns = lax.broadcasted_iota(jnp.int32, (T, T), 1)
    return jnp.sum(jnp.where(rows == columns, tile.astype(F32), 0.0), axis=0, keepdims=True)


def times_transposed(left, right):
    return lax.dot_general(left, right, (((1,), (1,)), ((), ())), preferred_element_type=F32)


def prepare_kernel(
    is_leaf, active, coupler, step_diagonal, inverse_far, step_far, links_far, _, __, factors, constants,
    inverse, step_inverse, first, second, lower, step, sems,
):
    @pl.when(active[0] == 1)
    def _():
        loads = [
            pltpu.make_async_copy(far, near, sems.at[i])
            for i, (far, near) in enumerate(
                [(links_far.at[0, 0], first), (inverse_far, inverse), (step_far, step_inverse), (links_far.at[0, 1], second)]
            )
        ]
        for copy in loads:
            copy.start()
        loads[0].wait()
        if is_leaf:
            factors[:, :B] = mm(coupler[...], first[...]).astype(BF)
        else:
            factors[:, :B] = first[...]
        loads[1].wait()
        if is_leaf:
            lower[...] = mm(inverse[...], first[...]).astype(BF)
            for i in range(TILES):
                constants[0:1, rows_of(i)] = diagonal_row(inverse, i * T, i * T)
        else:
            constants[0:1, :] = jnp.zeros((1, B), F32)
        loads[2].wait()
        if is_leaf:
            step[...] = step_inverse[...].astype(F32) + lax.dot_general(
                first[...], lower[...], (((0,), (0,)), ((), ())), preferred_element_type=F32
            )
        else:
            step[...] = step_inverse[...].astype(F32)
        for i in range(TILES):
            constants[1:2, rows_of(i)] = diagonal_row(step, i * T, i * T)
        loads[3].wait()
        factors[:, B:] = mm(factors[:, :B], second[...]).astype(BF)
        last = mm(step[...].astype(BF), second[...])
        extra = jnp.sum(second[...].astype(F32) * last, axis=0, keepdims=True) + step_diagonal[...]
        constants[2:3, :] = extra
        constants[3:8, :] = jnp.zeros((5, B), F32)


def prepare(is_leaf, active, coupler, step_diagonal, inverse, step_inverse, links, factors, constants):
    far = [pltpu.with_memory_space_constraint(a, pltpu.HBM) for a in (inverse, step_inverse, links)]
    block = pltpu.VMEM((B, B), BF)
    return pl.pallas_call(
        functools.partial(prepare_kernel, is_leaf),
        out_shape=(pltpu.VMEM((B, 2 * B), BF), pltpu.VMEM((8, B), F32)),
        in_specs=[SMEM, VMEM, VMEM, HBM, HBM, HBM, VMEM, VMEM],
        out_specs=(VMEM, VMEM),
        input_output_aliases={6: 0, 7: 1},
        scratch_shapes=[block, block, block, block, block, pltpu.VMEM((B, B), F32), pltpu.SemaphoreType.DMA((4,))],
        compiler_params=params(),
        cost_estimate=cost(5),
    )(active, coupler, step_diagonal, *far, factors, constants)


HEAD = 16
GATHERED = 4
ALL_ROWS = 8 << GATHERED


def halved(packed, i):
    row = packed[:, strip(i)]
    diagonal = row[:, :T] * BF(0.5)
    return diagonal if i == TILES - 1 else jnp.concatenate([diagonal, row[:, T:]], axis=1)


def block_forms(left, right):
    count = right.shape[0]
    high = left.astype(BF)
    low = (left - high.astype(F32)).astype(BF)
    gram = times_transposed(high, right) + times_transposed(low, right)
    rows = lax.broadcasted_iota(jnp.int32, (count, count), 0)
    columns = lax.broadcasted_iota(jnp.int32, (count, count), 1)
    gram = jnp.where(rows // 4 == columns // 4, gram, 0.0)
    folded = jnp.sum(gram.reshape(count // 8, 8, count), axis=0)
    folded = jnp.concatenate([folded[:4] + folded[4:], jnp.zeros((4, count), F32)], axis=0)
    if count < T:
        folded = jnp.concatenate([folded, jnp.zeros((8, T - count), F32)], axis=1)
    shift = T // 2
    while shift >= 4:
        folded = folded + pltpu.roll(folded, shift, 1)
        shift //= 2
    lanes = lax.broadcasted_iota(jnp.int32, (8, T), 1)
    return jnp.where(lanes < 4, folded, 0.0)


def packed_forms(rows, packed):
    parts = [mm(rows[:, rows_of(i)], halved(packed, i)) for i in range(TILES)]
    columns = []
    for i in range(TILES):
        column = parts[0][:, rows_of(i)]
        for k in range(1, i + 1):
            column = column + parts[k][:, (i - k) * T : (i - k + 1) * T]
        columns.append(column)
    form = block_forms(jnp.concatenate(columns, axis=1), rows)
    square = jnp.concatenate([form, jnp.zeros((T - 8, T), F32)], axis=0)
    return form + square.T[:8]


def write_constants(message, value):
    high = value.astype(BF).astype(F32)
    head = jnp.concatenate([high, value - high, jnp.zeros((8, T), F32)], axis=0)
    message[0:HEAD, 0:T] = head.astype(BF)


def constants_of(message):
    head = message[0:HEAD, 0:T].astype(F32)
    return jnp.concatenate([head[0:4] + head[4:8], jnp.zeros((4, T), F32)], axis=0)


def own_message_kernel(arrows, links_far, step_far, message, link, step_inverse, sems):
    fetch(sems, (links_far.at[0, 0], link), (step_far, step_inverse))
    a0 = arrows[0, 0]
    a1 = arrows[0, 1]
    through = times_transposed(a1, link[...])
    own = jnp.concatenate([a0.astype(F32), through, jnp.zeros((8, B), F32)], axis=0)
    message[HEAD:, :] = own.astype(BF)
    zeros = jnp.zeros((4, B), BF)
    padded = jnp.concatenate([a1, zeros, zeros, zeros], axis=0)
    write_constants(message, block_forms(mm(padded, step_inverse[...]), padded)[:4])


def own_message(arrows, links, step_inverse):
    return pl.pallas_call(
        own_message_kernel,
        out_shape=jax.ShapeDtypeStruct((HEAD + 16, B), BF),
        in_specs=[VMEM, HBM, HBM],
        out_specs=VMEM,
        scratch_shapes=[
            pltpu.VMEM((B, B), BF), pltpu.VMEM((B, B), BF), pltpu.SemaphoreType.DMA((2,)),
        ],
        compiler_params=params(),
        cost_estimate=cost(0.001),
    )(arrows, *[pltpu.with_memory_space_constraint(a, pltpu.HBM) for a in (links, step_inverse)])


def first_eight(message):
    return message[HEAD:, :].astype(F32)[:8]


HALF = ALL_ROWS // 2


def chip_rows_kernel(own, other, coupler, rows):
    rows[...] = jnp.zeros((HALF, B), BF)
    through = times_transposed(own[HEAD:, :], coupler[...])
    rows[0:16, :] = jnp.concatenate([first_eight(other), through[:8]], axis=0).astype(BF)


def chip_rows(own, other, coupler):
    return pl.pallas_call(
        chip_rows_kernel,
        out_shape=pltpu.VMEM((HALF, B), BF),
        in_specs=[VMEM] * 3,
        out_specs=VMEM,
        compiler_params=params(),
        cost_estimate=cost(0.2),
    )(own, other, coupler)


def chip_constants_kernel(own, other, inverse_far, sums, inverse, sems):
    fetch(sems, (inverse_far, inverse))
    mine = own[HEAD:, :]
    sums[...] = constants_of(own) + constants_of(other) + block_forms(mm(mine, inverse[...]), mine)


def chip_constants(own, other, inverse):
    return pl.pallas_call(
        chip_constants_kernel,
        out_shape=jax.ShapeDtypeStruct((8, T), F32),
        in_specs=[VMEM, VMEM, HBM],
        out_specs=VMEM,
        scratch_shapes=[pltpu.VMEM((B, B), BF), pltpu.SemaphoreType.DMA((1,))],
        compiler_params=params(),
        cost_estimate=cost(0.2),
    )(own, other, pltpu.with_memory_space_constraint(inverse, pltpu.HBM))


def up_kernel(stage, flags, coupler_any, incoming_any, _, rows, message, coupler, sems):
    if stage > 1:

        @pl.when(flags[0] == 1)
        def _():
            count = 8 << (stage - 1)
            fetch(sems, (incoming_any, rows.at[pl.ds(count, count)]))

    @pl.when(flags[1] == 1)
    def _():
        fetch(sems, (coupler_any, coupler))
        message[...] = times_transposed(rows[0 : 8 << stage, :], coupler[...]).astype(BF)


def up(stage, flags, coupler, incoming, rows):
    return pl.pallas_call(
        functools.partial(up_kernel, stage),
        out_shape=(pltpu.VMEM((HALF, B), BF), pltpu.VMEM((8 << stage, B), BF)),
        in_specs=[SMEM, ANY, ANY, VMEM],
        out_specs=(VMEM,) * 2,
        input_output_aliases={3: 0},
        scratch_shapes=[pltpu.VMEM((B, B), BF), pltpu.SemaphoreType.DMA((1,))],
        compiler_params=params(),
        cost_estimate=cost(0.3),
    )(flags, coupler, incoming, rows)


def finish_kernel(rows, out):
    out[...] = rows[...]


def finish(rows):
    return pl.pallas_call(
        finish_kernel,
        out_shape=jax.ShapeDtypeStruct(rows.shape, BF),
        in_specs=[VMEM],
        out_specs=VMEM,
        compiler_params=params(),
        cost_estimate=cost(0.1),
    )(rows)


def absorb_kernel(
    scale, flags, block_any, state_any, incoming_any, rows, sums, tip, block, incoming, sems
):
    def add_to_row(value):
        row = value[0:1]
        for j in range(1, 4):
            row = row + pltpu.roll(value[j : j + 1], 4 * j, 1)
        tip[...] = row * scale

    @pl.when(flags[0] == 1)
    def _():
        fetch(sems, (state_any, block), (incoming_any, incoming))
        add_to_row(sums[...] + packed_forms(rows[...], block) + packed_forms(incoming[...], block))

    @pl.when(flags[0] != 1)
    def _():
        fetch(sems, (block_any, block))
        add_to_row(sums[...] + packed_forms(rows[...], block))


def absorb(scale, flags, block_zero, state_zero, incoming, rows, sums):
    return pl.pallas_call(
        functools.partial(absorb_kernel, scale),
        out_shape=jax.ShapeDtypeStruct((1, T), F32),
        in_specs=[SMEM, ANY, ANY, ANY, VMEM, VMEM],
        out_specs=VMEM,
        scratch_shapes=[
            pltpu.VMEM((T, PACKED), BF), pltpu.VMEM(incoming.shape, BF), pltpu.SemaphoreType.DMA((2,)),
        ],
        compiler_params=params(),
        cost_estimate=cost(0.5),
    )(flags, block_zero, state_zero, incoming, rows, sums)


def tail_kernel(
    flags, received, state, coupler, factors, constants, tip, tip_received, variances, tip_out, source
):
    leaf = flags[0]

    @pl.when(leaf == 1)
    def _():
        source[...] = received[...]
        own = jnp.zeros((1, B), F32)
        for i in range(TILES):
            product = mm(halved(source, i), coupler[i * T :, :])
            own = own + jnp.sum(product * coupler[rows_of(i), :].astype(F32), axis=0, keepdims=True)
        variances[0] = constants[0:1, :] + 2.0 * own

    @pl.when(leaf != 1)
    def _():
        source[...] = state[...]
        for i in range(TILES):
            variances[0, :, rows_of(i)] = diagonal_row(state, 0, STARTS[i])

    total = jnp.zeros((1, 2 * B), F32)
    for i in range(TILES):
        product = mm(halved(source, i), factors[i * T :, :])
        total = total + jnp.sum(
            product * factors[rows_of(i), :].astype(F32), axis=0, keepdims=True
        )
    total = 2.0 * total
    variances[1] = constants[1:2, :] + total[:, :B]
    variances[2] = jnp.where(flags[1] == 2, constants[2:3, :] + total[:, B:], 0.0)
    row = jnp.where(leaf == 1, tip[...], tip_received[...])
    for j in range(4):
        turned = row if j == 0 else pltpu.roll(row, T - 4 * j, 1)
        tip_out[j : j + 1, :] = turned[:, 0:4]


def tail(flags, received, state, coupler, factors, constants, tip, tip_received):
    return pl.pallas_call(
        tail_kernel,
        out_shape=(
            jax.ShapeDtypeStruct((3, 1, B), F32),
            jax.ShapeDtypeStruct((4, 4), F32),
        ),
        in_specs=[SMEM] + [VMEM] * 7,
        out_specs=(VMEM, VMEM),
        scratch_shapes=[pltpu.VMEM((T, PACKED), BF)],
        compiler_params=params(),
        cost_estimate=cost(3),
    )(flags, received, state, coupler, factors, constants, tip, tip_received)


def blank_kernel(out):
    pass


def blank(shape, dtype, kind=jax.ShapeDtypeStruct):
    return pl.pallas_call(
        blank_kernel,
        out_shape=kind(shape, dtype),
        out_specs=VMEM if kind is pltpu.VMEM else ANY,
        compiler_params=params(),
        cost_estimate=cost(0.001),
    )()


def swap_pairs(devices, bit):
    return [(i, i ^ bit) for i in range(devices)]


def chip_cycles(devices, height):
    target = {i: i ^ 1 for i in range(devices)}
    for child in range(1 << height, devices, 2 << height):
        parent = child - (1 << height)
        target[parent] = child
        target[child] = child + 1
        target[child + 1] = parent + 1
        target[parent + 1] = parent
    return sorted(target.items())


def neighbour_cycles(devices, height, offset):
    target = {i: i ^ 1 for i in range(devices)}
    for child in range(1 << height, devices, 2 << height):
        for core in range(2):
            first, second = child - (1 << height) + core, child + core
            target[first] = second
            target[second] = second + offset
            target[second + offset] = first + offset
            target[first + offset] = first
    return sorted(target.items())


def children(devices, source, target):
    return [(row + 2 * source, row + 2 * target) for row in range(0, devices, 8)]


def row_cycles(devices, cycle):
    return [
        (row + 2 * cycle[k - 1] + core, row + 2 * cycle[k] + core)
        for row in range(0, devices, 8)
        for k in range(4)
        for core in range(2)
    ]


def summing_order(devices):
    def place(chip):
        layer = chip % 64 // 8
        early = layer if layer < 4 else 11 - layer
        if chip % (1 << GATHERED) == 0:
            return (1, early, chip // 64)
        return (0, -early, -(chip // 64), -(chip % 8))

    return sorted(range(0, devices, 2), key=place)


def after(arrays, *others):
    return lax.optimization_barrier((arrays, others))[0]


def integers(*values):
    return jnp.stack([jnp.asarray(value, jnp.int32) for value in values])


def shards(boundary_inverse, coupling, step_inverse, step_diagonal, links, arrows, lengths):
    blocks = lax.axis_size("tm")
    me = lax.axis_index("tm")
    chip = me - me % 2
    on_core_one = me % 2 == 1
    inverse = boundary_inverse[0]
    step_inv = step_inverse[0]
    swap = swap_pairs(blocks, 1)
    absorbs = chip % (1 << GATHERED) == 0

    def send(array, pairs):
        return lax.ppermute(array, "tm", pairs)

    def descend(height, parent, state):
        active = integers(me % (2 << height) == 1 << height)
        return level(active, parent, coupler, turned, state)

    def helper(height):
        return 6 if height % 2 else 2

    def takes_part(height):
        place = me % (1 << height)
        return (place == 0) | (place == helper(height))

    def is_sender(stage):
        return chip % (2 << stage) == 1 << stage

    def is_receiver(stage):
        return chip % (2 << stage) == 0

    state = pack(inverse)

    parent = send(state, chip_cycles(blocks, 7))
    given = after((arrows, links, step_inv), state)
    mine = own_message(*given)
    factors = blank((B, 2 * B), BF, pltpu.VMEM)
    constants = blank((8, B), F32, pltpu.VMEM)
    coupler, turned = open_coupler(after(coupling[0], mine))
    coupler_zero = send(coupling[0], swap)
    message_zero = send(mine, swap)
    block_zero = parent
    parent, coupler_zero, message_zero = lax.optimization_barrier((parent, coupler_zero, message_zero))
    state = descend(7, parent, state)

    def get_ready(is_leaf, active, factors, constants, *others):
        given = after((step_diagonal, inverse, step_inv, links), *others)
        return list(prepare(is_leaf, integers(active), coupler, *given, factors, constants))

    def tree_top(state, factors, constants):
        factors, constants = get_ready(False, chip % 64 != 0, factors, constants)
        for height in (6, 5, 4):
            state = lax.cond(
                takes_part(height),
                lambda s, h=height: descend(h, send(s, neighbour_cycles(blocks, h, helper(h))), s),
                lambda s: s,
                state,
            )
        return [state, blank((HALF, B), BF), blank((HALF, B), BF), blank((8, T), F32), factors, constants]

    def gather_rows(state, factors, constants):
        rows = chip_rows(mine, message_zero, coupler)
        message = message_zero
        sums = None
        for stage in range(1, GATHERED):
            flags = integers(is_receiver(stage - 1), is_sender(stage))
            rows, message = up(stage, flags, coupler_zero, message, rows)
            message = send(message, swap_pairs(blocks, 1 << stage))
            if sums is None:
                sums = chip_constants(mine, message_zero, after(inverse, rows))
                message, sums = lax.optimization_barrier((message, sums))
        rows = finish(rows)
        return [state, rows, message, sums, *get_ready(True, 1, factors, constants, message)]

    state, rows, message, sums, factors, constants = lax.cond(
        on_core_one, gather_rows, tree_top, state, factors, constants
    )

    def middle(state, factors, constants):
        parent = send(copied(state), chip_cycles(blocks, 3))
        state_zero = send(state, swap)
        factors, constants = get_ready(False, me % 64 == 0, factors, constants, state)
        parent, state_zero, factors, constants = lax.optimization_barrier(
            (parent, state_zero, factors, constants)
        )
        return [descend(3, parent, state), state_zero, factors, constants]

    state, state_zero, factors, constants = lax.cond(
        chip % 8 == 0, middle, lambda s, f, c: [s, blank((T, PACKED), BF), f, c], state, factors, constants
    )

    def sum_tips(state):
        tip = absorb(1.0 / (2 * blocks), integers(absorbs), block_zero, state_zero, message, rows, sums)
        every = lax.all_to_all(
            jnp.broadcast_to(tip[None], (blocks // 2, 1, T)), "tm", 0, 0,
            axis_index_groups=[[chip + core for chip in summing_order(blocks)] for core in range(2)],
        )
        return [state, jnp.sum(every, axis=0)]

    def tree_bottom(state):
        place = me % 8
        to_third = send(copied(state), row_cycles(blocks, (0, 2, 3, 1)))
        to_second = send(state, children(blocks, 0, 1))
        to_third, before = lax.optimization_barrier((to_third, state))
        state = level(integers(place == 4), to_third, coupler, turned, before)
        to_fourth = send(state, children(blocks, 2, 3))
        state = level(integers(place == 2), after(to_second, state), coupler, turned, state)
        state = level(integers(place == 6), to_fourth, coupler, turned, state)
        return [state, blank((1, T), F32)]

    state, tip = lax.cond(on_core_one, sum_tips, tree_bottom, state)
    parent = send(state, swap)
    tip_received = send(tip, swap)
    flags = integers(me % 2, lengths[0])
    variances, total = tail(flags, parent, state, coupler, factors, constants, tip, tip_received)
    return jnp.transpose(variances, (1, 0, 2)), total


def solution(mesh):
    in_specs = (
        P("tm", None, None),
        P("tm", None, None),
        P("tm", None, None),
        P("tm", None),
        P("tm", None, None, None),
        P("tm", None, None, None),
        P("tm"),
    )
    out_specs = (P("tm", None, None), P())
    return jax.shard_map(shards, mesh=mesh, in_specs=in_specs, out_specs=out_specs, check_vma=False)
```

```python
import functools

import jax
import jax.numpy as jnp
from jax import lax
from jax.experimental import pallas as pl
from jax.experimental.pallas import tpu as pltpu
from jax.sharding import PartitionSpec as P

B = 512
T = 128
TILES = B // T
STARTS = [0, 4 * T, 7 * T, 9 * T]
WIDTHS = [4 * T, 3 * T, 2 * T, T]
PACKED = 10 * T
BF = jnp.bfloat16
F32 = jnp.float32

VMEM = pl.BlockSpec(memory_space=pltpu.VMEM)
SMEM = pl.BlockSpec(memory_space=pltpu.SMEM)
ANY = pl.BlockSpec(memory_space=pl.ANY)
HBM = pl.BlockSpec(memory_space=pltpu.HBM)


def strip(i):
    return slice(STARTS[i], STARTS[i] + WIDTHS[i])


def rows_of(i):
    return slice(i * T, (i + 1) * T)


def mm(a, b):
    return jnp.dot(a, b, preferred_element_type=F32)


def fetch(sems, *pairs):
    copies = [pltpu.make_async_copy(a, b, sems.at[i]) for i, (a, b) in enumerate(pairs)]
    for copy in copies:
        copy.start()
    for copy in copies:
        copy.wait()


def params():
    return pltpu.CompilerParams(vmem_limit_bytes=12 * 2**20)


def cost(products):
    return pl.CostEstimate(
        flops=int(products * 2 * B**3), bytes_accessed=int(min(products, 1) * 4 * B * B), transcendentals=0
    )


def pack_kernel(full, packed, sems):
    fetch(
        sems,
        *[
            (full.at[pl.ds(i * T, T), pl.ds(i * T, WIDTHS[i])], packed.at[:, pl.ds(STARTS[i], WIDTHS[i])])
            for i in range(TILES)
        ],
    )


def pack(full):
    return pl.pallas_call(
        pack_kernel,
        out_shape=pltpu.VMEM((T, PACKED), BF),
        in_specs=[HBM],
        out_specs=VMEM,
        scratch_shapes=[pltpu.SemaphoreType.DMA((TILES,))],
        compiler_params=params(),
        cost_estimate=cost(0.01),
    )(pltpu.with_memory_space_constraint(full, pltpu.HBM))


def open_kernel(coupling, coupler, turned, sems):
    fetch(sems, (coupling, coupler))
    turned[...] = coupler[...].T


def open_coupler(coupling):
    block = pltpu.VMEM((B, B), BF)
    return pl.pallas_call(
        open_kernel,
        out_shape=(block, block),
        in_specs=[HBM],
        out_specs=(VMEM,) * 2,
        scratch_shapes=[pltpu.SemaphoreType.DMA((1,))],
        compiler_params=params(),
        cost_estimate=cost(0.001),
    )(pltpu.with_memory_space_constraint(coupling, pltpu.HBM))


def copy_kernel(a, out):
    out[...] = a[...]


def copied(a):
    return pl.pallas_call(
        copy_kernel,
        out_shape=pltpu.VMEM(a.shape, a.dtype),
        in_specs=[VMEM],
        out_specs=VMEM,
        compiler_params=params(),
        cost_estimate=cost(0.5),
    )(a)


def unpack(packed, full):
    for i in range(TILES):
        row = packed[:, strip(i)]
        full[rows_of(i), i * T :] = row
        for j in range(i + 1, TILES):
            full[rows_of(j), rows_of(i)] = row[:, (j - i) * T : (j - i + 1) * T].T


def level_kernel(active, parent, coupler, coupler_t, state, state_out, full, bridge):
    @pl.when(active[0] == 1)
    def _():
        unpack(parent, full)
        bridge[...] = mm(full[...], coupler[...]).astype(BF)
        for i in range(TILES):
            fresh = mm(coupler_t[rows_of(i), :], bridge[:, i * T :])
            state_out[:, strip(i)] = (state[:, strip(i)].astype(F32) + fresh).astype(BF)


def level(active, parent, coupler, coupler_t, state):
    return pl.pallas_call(
        level_kernel,
        out_shape=pltpu.VMEM((T, PACKED), BF),
        in_specs=[SMEM] + [VMEM] * 4,
        out_specs=VMEM,
        input_output_aliases={4: 0},
        scratch_shapes=[pltpu.VMEM((B, B), BF), pltpu.VMEM((B, B), BF)],
        compiler_params=params(),
        cost_estimate=cost(2),
    )(active, parent, coupler, coupler_t, state)


def diagonal_row(a, top, left):
    tile = a[top : top + T, left : left + T]
    rows = lax.broadcasted_iota(jnp.int32, (T, T), 0)
    columns = lax.broadcasted_iota(jnp.int32, (T, T), 1)
    return jnp.sum(jnp.where(rows == columns, tile.astype(F32), 0.0), axis=0, keepdims=True)


def times_transposed(left, right):
    return lax.dot_general(left, right, (((1,), (1,)), ((), ())), preferred_element_type=F32)


def prepare_kernel(
    is_leaf, active, coupler, step_diagonal, inverse_far, step_far, links_far, _, __, factors, constants,
    inverse, step_inverse, first, second, lower, step, sems,
):
    @pl.when(active[0] == 1)
    def _():
        loads = [
            pltpu.make_async_copy(far, near, sems.at[i])
            for i, (far, near) in enumerate(
                [(links_far.at[0, 0], first), (inverse_far, inverse), (step_far, step_inverse), (links_far.at[0, 1], second)]
            )
        ]
        for copy in loads:
            copy.start()
        loads[0].wait()
        if is_leaf:
            factors[:, :B] = mm(coupler[...], first[...]).astype(BF)
        else:
            factors[:, :B] = first[...]
        loads[1].wait()
        if is_leaf:
            lower[...] = mm(inverse[...], first[...]).astype(BF)
            for i in range(TILES):
                constants[0:1, rows_of(i)] = diagonal_row(inverse, i * T, i * T)
        else:
            constants[0:1, :] = jnp.zeros((1, B), F32)
        loads[2].wait()
        if is_leaf:
            step[...] = step_inverse[...].astype(F32) + lax.dot_general(
                first[...], lower[...], (((0,), (0,)), ((), ())), preferred_element_type=F32
            )
        else:
            step[...] = step_inverse[...].astype(F32)
        for i in range(TILES):
            constants[1:2, rows_of(i)] = diagonal_row(step, i * T, i * T)
        loads[3].wait()
        factors[:, B:] = mm(factors[:, :B], second[...]).astype(BF)
        last = mm(step[...].astype(BF), second[...])
        extra = jnp.sum(second[...].astype(F32) * last, axis=0, keepdims=True) + step_diagonal[...]
        constants[2:3, :] = extra
        constants[3:4, :] = jnp.full((1, B), float(is_leaf), F32)
        constants[4:8, :] = jnp.zeros((4, B), F32)


def prepare(is_leaf, active, coupler, step_diagonal, inverse, step_inverse, links, factors, constants):
    far = [pltpu.with_memory_space_constraint(a, pltpu.HBM) for a in (inverse, step_inverse, links)]
    block = pltpu.VMEM((B, B), BF)
    return pl.pallas_call(
        functools.partial(prepare_kernel, is_leaf),
        out_shape=(pltpu.VMEM((B, 2 * B), BF), pltpu.VMEM((8, B), F32)),
        in_specs=[SMEM, VMEM, VMEM, HBM, HBM, HBM, VMEM, VMEM],
        out_specs=(VMEM, VMEM),
        input_output_aliases={6: 0, 7: 1},
        scratch_shapes=[block, block, block, block, block, pltpu.VMEM((B, B), F32), pltpu.SemaphoreType.DMA((4,))],
        compiler_params=params(),
        cost_estimate=cost(5),
    )(active, coupler, step_diagonal, *far, factors, constants)


HEAD = 16
GATHERED = 4
ALL_ROWS = 8 << GATHERED


def halved(packed, i):
    row = packed[:, strip(i)]
    diagonal = row[:, :T] * BF(0.5)
    return diagonal if i == TILES - 1 else jnp.concatenate([diagonal, row[:, T:]], axis=1)


def block_forms(left, right):
    count = right.shape[0]
    high = left.astype(BF)
    low = (left - high.astype(F32)).astype(BF)
    gram = times_transposed(high, right) + times_transposed(low, right)
    rows = lax.broadcasted_iota(jnp.int32, (count, count), 0)
    columns = lax.broadcasted_iota(jnp.int32, (count, count), 1)
    gram = jnp.where(rows // 4 == columns // 4, gram, 0.0)
    folded = jnp.sum(gram.reshape(count // 8, 8, count), axis=0)
    folded = jnp.concatenate([folded[:4] + folded[4:], jnp.zeros((4, count), F32)], axis=0)
    if count < T:
        folded = jnp.concatenate([folded, jnp.zeros((8, T - count), F32)], axis=1)
    shift = T // 2
    while shift >= 4:
        folded = folded + pltpu.roll(folded, shift, 1)
        shift //= 2
    lanes = lax.broadcasted_iota(jnp.int32, (8, T), 1)
    return jnp.where(lanes < 4, folded, 0.0)


def packed_forms(rows, packed):
    parts = [mm(rows[:, rows_of(i)], halved(packed, i)) for i in range(TILES)]
    columns = []
    for i in range(TILES):
        column = parts[0][:, rows_of(i)]
        for k in range(1, i + 1):
            column = column + parts[k][:, (i - k) * T : (i - k + 1) * T]
        columns.append(column)
    form = block_forms(jnp.concatenate(columns, axis=1), rows)
    square = jnp.concatenate([form, jnp.zeros((T - 8, T), F32)], axis=0)
    return form + square.T[:8]


def write_constants(message, value):
    high = value.astype(BF).astype(F32)
    head = jnp.concatenate([high, value - high, jnp.zeros((8, T), F32)], axis=0)
    message[0:HEAD, 0:T] = head.astype(BF)


def constants_of(message):
    head = message[0:HEAD, 0:T].astype(F32)
    return jnp.concatenate([head[0:4] + head[4:8], jnp.zeros((4, T), F32)], axis=0)


def own_message_kernel(arrows, links_far, step_far, live_any, message, steps, link, step_inverse, live, sems):
    fetch(sems, (links_far.at[0, 0], link), (step_far, step_inverse), (live_any, live))
    steps[...] = jnp.full((8, T), live[0], jnp.int32).astype(F32)
    a0 = arrows[0, 0]
    a1 = arrows[0, 1]
    through = times_transposed(a1, link[...])
    own = jnp.concatenate([a0.astype(F32), through, jnp.zeros((8, B), F32)], axis=0)
    message[HEAD:, :] = own.astype(BF)
    zeros = jnp.zeros((4, B), BF)
    padded = jnp.concatenate([a1, zeros, zeros, zeros], axis=0)
    write_constants(message, block_forms(mm(padded, step_inverse[...]), padded)[:4])


def own_message(arrows, links, step_inverse, lengths):
    return pl.pallas_call(
        own_message_kernel,
        out_shape=(jax.ShapeDtypeStruct((HEAD + 16, B), BF), pltpu.VMEM((8, T), F32)),
        in_specs=[VMEM, HBM, HBM, ANY],
        out_specs=(VMEM, VMEM),
        scratch_shapes=[
            pltpu.VMEM((B, B), BF), pltpu.VMEM((B, B), BF), pltpu.SMEM((1,), jnp.int32),
            pltpu.SemaphoreType.DMA((3,)),
        ],
        compiler_params=params(),
        cost_estimate=cost(0.001),
    )(arrows, *[pltpu.with_memory_space_constraint(a, pltpu.HBM) for a in (links, step_inverse)], lengths)


def first_eight(message):
    return message[HEAD:, :].astype(F32)[:8]


HALF = ALL_ROWS // 2


def chip_rows_kernel(own, other, coupler, rows):
    rows[...] = jnp.zeros((HALF, B), BF)
    through = times_transposed(own[HEAD:, :], coupler[...])
    rows[0:16, :] = jnp.concatenate([first_eight(other), through[:8]], axis=0).astype(BF)


def chip_rows(own, other, coupler):
    return pl.pallas_call(
        chip_rows_kernel,
        out_shape=pltpu.VMEM((HALF, B), BF),
        in_specs=[VMEM] * 3,
        out_specs=VMEM,
        compiler_params=params(),
        cost_estimate=cost(0.2),
    )(own, other, coupler)


def chip_constants_kernel(own, other, inverse_far, sums, inverse, sems):
    fetch(sems, (inverse_far, inverse))
    mine = own[HEAD:, :]
    sums[...] = constants_of(own) + constants_of(other) + block_forms(mm(mine, inverse[...]), mine)


def chip_constants(own, other, inverse):
    return pl.pallas_call(
        chip_constants_kernel,
        out_shape=jax.ShapeDtypeStruct((8, T), F32),
        in_specs=[VMEM, VMEM, HBM],
        out_specs=VMEM,
        scratch_shapes=[pltpu.VMEM((B, B), BF), pltpu.SemaphoreType.DMA((1,))],
        compiler_params=params(),
        cost_estimate=cost(0.2),
    )(own, other, pltpu.with_memory_space_constraint(inverse, pltpu.HBM))


def up_kernel(stage, flags, coupler_any, incoming_any, _, rows, message, coupler, sems):
    if stage > 1:

        @pl.when(flags[0] == 1)
        def _():
            count = 8 << (stage - 1)
            fetch(sems, (incoming_any, rows.at[pl.ds(count, count)]))

    @pl.when(flags[1] == 1)
    def _():
        fetch(sems, (coupler_any, coupler))
        message[...] = times_transposed(rows[0 : 8 << stage, :], coupler[...]).astype(BF)


def up(stage, flags, coupler, incoming, rows):
    return pl.pallas_call(
        functools.partial(up_kernel, stage),
        out_shape=(pltpu.VMEM((HALF, B), BF), pltpu.VMEM((8 << stage, B), BF)),
        in_specs=[SMEM, ANY, ANY, VMEM],
        out_specs=(VMEM,) * 2,
        input_output_aliases={3: 0},
        scratch_shapes=[pltpu.VMEM((B, B), BF), pltpu.SemaphoreType.DMA((1,))],
        compiler_params=params(),
        cost_estimate=cost(0.3),
    )(flags, coupler, incoming, rows)


def finish_kernel(rows, out):
    out[...] = rows[...]


def finish(rows):
    return pl.pallas_call(
        finish_kernel,
        out_shape=jax.ShapeDtypeStruct(rows.shape, BF),
        in_specs=[VMEM],
        out_specs=VMEM,
        compiler_params=params(),
        cost_estimate=cost(0.1),
    )(rows)


def absorb_kernel(
    scale, flags, block_any, state_any, incoming_any, rows, sums, tips, block, gathered, sems
):
    gathered[0:HALF, :] = rows[...]

    @pl.when(flags[0] == 1)
    def _():
        fetch(sems, (state_any, block), (incoming_any, gathered.at[pl.ds(HALF, HALF)]))

    @pl.when(flags[0] != 1)
    def _():
        gathered[HALF:, :] = jnp.zeros((HALF, B), BF)
        fetch(sems, (block_any, block))

    value = sums[...] + packed_forms(gathered[...], block)
    row = value[0:1]
    for j in range(1, 4):
        row = row + pltpu.roll(value[j : j + 1], 4 * j, 1)
    tips[...] = jnp.broadcast_to((row * scale)[None], tips.shape)


def absorb(scale, flags, block_zero, state_zero, incoming, rows, sums, copies):
    return pl.pallas_call(
        functools.partial(absorb_kernel, scale),
        out_shape=jax.ShapeDtypeStruct((copies, 1, T), F32),
        in_specs=[SMEM, ANY, ANY, ANY, VMEM, VMEM],
        out_specs=VMEM,
        scratch_shapes=[
            pltpu.VMEM((T, PACKED), BF), pltpu.VMEM((ALL_ROWS, B), BF), pltpu.SemaphoreType.DMA((2,)),
        ],
        compiler_params=params(),
        cost_estimate=cost(0.5),
    )(flags, block_zero, state_zero, incoming, rows, sums)


def tail_kernel(
    received, state, coupler, factors, constants, steps, tip, tip_received, variances, tip_out
):
    leaf = constants[3:4, 0:1] == 1.0
    totals = [jnp.zeros((8, B), F32) for _ in range(3)]
    for i in range(TILES):
        row = jnp.where(leaf, received[:, strip(i)].astype(F32), state[:, strip(i)].astype(F32))
        halves = [row[:, :T] * 0.5, row[:, T:]]
        upper = jnp.concatenate(halves[: 2 if i < TILES - 1 else 1], axis=1).astype(BF)
        for k, (block, start) in enumerate(((coupler, 0), (factors, 0), (factors, B))):
            product = mm(upper, block[i * T :, start : start + B])
            terms = product * block[rows_of(i), start : start + B].astype(F32)
            totals[k] = totals[k] + jnp.sum(terms.reshape(T // 8, 8, B), axis=0)
    values = [
        constants[k : k + 1, :] + 2.0 * jnp.sum(total, axis=0, keepdims=True)
        for k, total in enumerate(totals)
    ]
    for i in range(TILES):
        own = diagonal_row(state, 0, STARTS[i])
        variances[0, :, rows_of(i)] = jnp.where(leaf, values[0][:, rows_of(i)], own)
    variances[1] = values[1]
    variances[2] = jnp.where(steps[0:1, 0:1] == 2.0, values[2], 0.0)
    row = jnp.where(leaf, tip[...], tip_received[...])
    for j in range(4):
        turned = row if j == 0 else pltpu.roll(row, T - 4 * j, 1)
        tip_out[j : j + 1, :] = turned[:, 0:4]


def tail(received, state, coupler, factors, constants, steps, tip, tip_received):
    return pl.pallas_call(
        tail_kernel,
        out_shape=(
            jax.ShapeDtypeStruct((3, 1, B), F32),
            jax.ShapeDtypeStruct((4, 4), F32),
        ),
        in_specs=[VMEM] * 8,
        out_specs=(VMEM, VMEM),
        compiler_params=params(),
        cost_estimate=cost(3),
    )(received, state, coupler, factors, constants, steps, tip, tip_received)


def blank_kernel(out):
    pass


def blank(shape, dtype, kind=jax.ShapeDtypeStruct):
    return pl.pallas_call(
        blank_kernel,
        out_shape=kind(shape, dtype),
        out_specs=VMEM if kind is pltpu.VMEM else ANY,
        compiler_params=params(),
        cost_estimate=cost(0.001),
    )()


def swap_pairs(devices, bit):
    return [(i, i ^ bit) for i in range(devices)]


def chip_cycles(devices, height):
    target = {i: i ^ 1 for i in range(devices)}
    for child in range(1 << height, devices, 2 << height):
        parent = child - (1 << height)
        target[parent] = child
        target[child] = child + 1
        target[child + 1] = parent + 1
        target[parent + 1] = parent
    return sorted(target.items())


def neighbour_cycles(devices, height, offset):
    target = {i: i ^ 1 for i in range(devices)}
    for child in range(1 << height, devices, 2 << height):
        for core in range(2):
            first, second = child - (1 << height) + core, child + core
            target[first] = second
            target[second] = second + offset
            target[second + offset] = first + offset
            target[first + offset] = first
    return sorted(target.items())


def children(devices, source, target):
    return [(row + 2 * source, row + 2 * target) for row in range(0, devices, 8)]


def row_cycles(devices, cycle):
    return [
        (row + 2 * cycle[k - 1] + core, row + 2 * cycle[k] + core)
        for row in range(0, devices, 8)
        for k in range(4)
        for core in range(2)
    ]


def summing_order(devices):
    def place(chip):
        layer = chip % 64 // 8
        early = layer if layer < 4 else 11 - layer
        if chip % (1 << GATHERED) == 0:
            return (1, early, chip // 64)
        return (0, -early, -(chip // 64), -(chip % 8))

    return sorted(range(0, devices, 2), key=place)


def after(arrays, *others):
    return lax.optimization_barrier((arrays, others))[0]


def integers(*values):
    return jnp.stack([jnp.asarray(value, jnp.int32) for value in values])


def shards(boundary_inverse, coupling, step_inverse, step_diagonal, links, arrows, lengths):
    blocks = lax.axis_size("tm")
    me = lax.axis_index("tm")
    chip = me - me % 2
    on_core_one = me % 2 == 1
    inverse = boundary_inverse[0]
    step_inv = step_inverse[0]
    swap = swap_pairs(blocks, 1)
    absorbs = chip % (1 << GATHERED) == 0

    def send(array, pairs):
        return lax.ppermute(array, "tm", pairs)

    def descend(height, parent, state):
        active = integers(me % (2 << height) == 1 << height)
        return level(active, parent, coupler, turned, state)

    def helper(height):
        return 6 if height % 2 else 2

    def takes_part(height):
        place = me % (1 << height)
        return (place == 0) | (place == helper(height))

    def is_sender(stage):
        return chip % (2 << stage) == 1 << stage

    def is_receiver(stage):
        return chip % (2 << stage) == 0

    state = pack(inverse)

    parent = send(state, chip_cycles(blocks, 7))
    given = after((arrows, links, step_inv), state)
    mine, steps = own_message(*given, lengths)
    factors = blank((B, 2 * B), BF, pltpu.VMEM)
    constants = blank((8, B), F32, pltpu.VMEM)
    coupler, turned = open_coupler(after(coupling[0], mine))
    coupler_zero = send(coupling[0], swap)
    message_zero = send(mine, swap)
    block_zero = parent
    parent, coupler_zero, message_zero = lax.optimization_barrier((parent, coupler_zero, message_zero))
    state = descend(7, parent, state)

    def get_ready(is_leaf, active, factors, constants, *others):
        given = after((step_diagonal, inverse, step_inv, links), *others)
        return list(prepare(is_leaf, integers(active), coupler, *given, factors, constants))

    def tree_top(state, factors, constants):
        factors, constants = get_ready(False, chip % 64 != 0, factors, constants)
        for height in (6, 5, 4):
            state = lax.cond(
                takes_part(height),
                lambda s, h=height: descend(h, send(s, neighbour_cycles(blocks, h, helper(h))), s),
                lambda s: s,
                state,
            )
        return [state, blank((HALF, B), BF), blank((HALF, B), BF), blank((8, T), F32), factors, constants]

    def gather_rows(state, factors, constants):
        rows = chip_rows(mine, message_zero, coupler)
        message = message_zero
        sums = None
        for stage in range(1, GATHERED):
            flags = integers(is_receiver(stage - 1), is_sender(stage))
            rows, message = up(stage, flags, coupler_zero, message, rows)
            message = send(message, swap_pairs(blocks, 1 << stage))
            if sums is None:
                sums = chip_constants(mine, message_zero, after(inverse, rows))
                message, sums = lax.optimization_barrier((message, sums))
        rows = finish(rows)
        return [state, rows, message, sums, *get_ready(True, 1, factors, constants, message)]

    state, rows, message, sums, factors, constants = lax.cond(
        on_core_one, gather_rows, tree_top, state, factors, constants
    )

    def middle(state, factors, constants):
        parent = send(copied(state), chip_cycles(blocks, 3))
        state_zero = send(state, swap)
        factors, constants = get_ready(False, me % 64 == 0, factors, constants, state)
        parent, state_zero, factors, constants = lax.optimization_barrier(
            (parent, state_zero, factors, constants)
        )
        return [descend(3, parent, state), state_zero, factors, constants]

    state, state_zero, factors, constants = lax.cond(
        chip % 8 == 0, middle, lambda s, f, c: [s, blank((T, PACKED), BF), f, c], state, factors, constants
    )

    def sum_tips(state):
        tips = absorb(
            1.0 / (2 * blocks), integers(absorbs), block_zero, state_zero, message, rows, sums, blocks // 2
        )
        every = lax.all_to_all(
            tips, "tm", 0, 0,
            axis_index_groups=[[chip + core for chip in summing_order(blocks)] for core in range(2)],
        )
        return [state, jnp.sum(every, axis=0)]

    def tree_bottom(state):
        place = me % 8
        to_third = send(copied(state), row_cycles(blocks, (0, 2, 3, 1)))
        to_second = send(state, children(blocks, 0, 1))
        to_third, before = lax.optimization_barrier((to_third, state))
        state = level(integers(place == 4), to_third, coupler, turned, before)
        to_fourth = send(state, children(blocks, 2, 3))
        state = level(integers(place == 2), after(to_second, state), coupler, turned, state)
        state = level(integers(place == 6), to_fourth, coupler, turned, state)
        return [state, blank((1, T), F32)]

    state, tip = lax.cond(on_core_one, sum_tips, tree_bottom, state)
    parent = lax.cond(absorbs, lambda s, z: z, lambda s, z: send(s, swap), state, state_zero)
    tip_received = send(tip, swap)
    variances, total = tail(parent, state, coupler, factors, constants, steps, tip, tip_received)
    return jnp.transpose(variances, (1, 0, 2)), total


def solution(mesh):
    in_specs = (
        P("tm", None, None),
        P("tm", None, None),
        P("tm", None, None),
        P("tm", None),
        P("tm", None, None, None),
        P("tm", None, None, None),
        P("tm"),
    )
    out_specs = (P("tm", None, None), P())
    return jax.shard_map(shards, mesh=mesh, in_specs=in_specs, out_specs=out_specs, check_vma=False)
```

```python
import functools

import jax
import jax.numpy as jnp
from jax import lax
from jax.experimental import pallas as pl
from jax.experimental.pallas import tpu as pltpu
from jax.sharding import PartitionSpec as P

B = 512
T = 128
TILES = B // T
STARTS = [0, 4 * T, 7 * T, 9 * T]
WIDTHS = [4 * T, 3 * T, 2 * T, T]
PACKED = 10 * T
BF = jnp.bfloat16
F32 = jnp.float32

VMEM = pl.BlockSpec(memory_space=pltpu.VMEM)
SMEM = pl.BlockSpec(memory_space=pltpu.SMEM)
ANY = pl.BlockSpec(memory_space=pl.ANY)
HBM = pl.BlockSpec(memory_space=pltpu.HBM)


def strip(i):
    return slice(STARTS[i], STARTS[i] + WIDTHS[i])


def rows_of(i):
    return slice(i * T, (i + 1) * T)


def mm(a, b):
    return jnp.dot(a, b, preferred_element_type=F32)


def fetch(sems, *pairs):
    copies = [pltpu.make_async_copy(a, b, sems.at[i]) for i, (a, b) in enumerate(pairs)]
    for copy in copies:
        copy.start()
    for copy in copies:
        copy.wait()


def params():
    return pltpu.CompilerParams(vmem_limit_bytes=12 * 2**20)


def cost(products):
    return pl.CostEstimate(
        flops=int(products * 2 * B**3), bytes_accessed=int(min(products, 1) * 4 * B * B), transcendentals=0
    )


def pack_kernel(full, packed, sems):
    fetch(
        sems,
        *[
            (full.at[pl.ds(i * T, T), pl.ds(i * T, WIDTHS[i])], packed.at[:, pl.ds(STARTS[i], WIDTHS[i])])
            for i in range(TILES)
        ],
    )


def pack(full):
    return pl.pallas_call(
        pack_kernel,
        out_shape=pltpu.VMEM((T, PACKED), BF),
        in_specs=[HBM],
        out_specs=VMEM,
        scratch_shapes=[pltpu.SemaphoreType.DMA((TILES,))],
        compiler_params=params(),
        cost_estimate=cost(0.01),
    )(pltpu.with_memory_space_constraint(full, pltpu.HBM))


def open_kernel(coupling, coupler, turned, sems):
    fetch(sems, (coupling, coupler))
    turned[...] = coupler[...].T


def open_coupler(coupling):
    block = pltpu.VMEM((B, B), BF)
    return pl.pallas_call(
        open_kernel,
        out_shape=(block, block),
        in_specs=[HBM],
        out_specs=(VMEM,) * 2,
        scratch_shapes=[pltpu.SemaphoreType.DMA((1,))],
        compiler_params=params(),
        cost_estimate=cost(0.001),
    )(pltpu.with_memory_space_constraint(coupling, pltpu.HBM))


def copy_kernel(a, out):
    out[...] = a[...]


def copied(a):
    return pl.pallas_call(
        copy_kernel,
        out_shape=pltpu.VMEM(a.shape, a.dtype),
        in_specs=[VMEM],
        out_specs=VMEM,
        compiler_params=params(),
        cost_estimate=cost(0.5),
    )(a)


def unpack(packed, full):
    for i in range(TILES):
        row = packed[:, strip(i)]
        full[rows_of(i), i * T :] = row
        for j in range(i + 1, TILES):
            full[rows_of(j), rows_of(i)] = row[:, (j - i) * T : (j - i + 1) * T].T


def level_kernel(active, parent, coupler, coupler_t, state, state_out, full, bridge):
    @pl.when(active[0] == 1)
    def _():
        unpack(parent, full)
        bridge[...] = mm(full[...], coupler[...]).astype(BF)
        for i in range(TILES):
            fresh = mm(coupler_t[rows_of(i), :], bridge[:, i * T :])
            state_out[:, strip(i)] = (state[:, strip(i)].astype(F32) + fresh).astype(BF)


def level(active, parent, coupler, coupler_t, state):
    return pl.pallas_call(
        level_kernel,
        out_shape=pltpu.VMEM((T, PACKED), BF),
        in_specs=[SMEM] + [VMEM] * 4,
        out_specs=VMEM,
        input_output_aliases={4: 0},
        scratch_shapes=[pltpu.VMEM((B, B), BF), pltpu.VMEM((B, B), BF)],
        compiler_params=params(),
        cost_estimate=cost(2),
    )(active, parent, coupler, coupler_t, state)


def diagonal_row(a, top, left):
    tile = a[top : top + T, left : left + T]
    rows = lax.broadcasted_iota(jnp.int32, (T, T), 0)
    columns = lax.broadcasted_iota(jnp.int32, (T, T), 1)
    return jnp.sum(jnp.where(rows == columns, tile.astype(F32), 0.0), axis=0, keepdims=True)


def times_transposed(left, right):
    return lax.dot_general(left, right, (((1,), (1,)), ((), ())), preferred_element_type=F32)


def prepare_kernel(
    is_leaf, active, coupler, step_diagonal, inverse_far, step_far, links_far, _, __, factors, constants,
    inverse, step_inverse, first, second, lower, step, sems,
):
    @pl.when(active[0] == 1)
    def _():
        loads = [
            pltpu.make_async_copy(far, near, sems.at[i])
            for i, (far, near) in enumerate(
                [(links_far.at[0, 0], first), (inverse_far, inverse), (step_far, step_inverse), (links_far.at[0, 1], second)]
            )
        ]
        for copy in loads:
            copy.start()
        loads[0].wait()
        if is_leaf:
            factors[:, :B] = mm(coupler[...], first[...]).astype(BF)
        else:
            factors[:, :B] = first[...]
        loads[1].wait()
        if is_leaf:
            lower[...] = mm(inverse[...], first[...]).astype(BF)
            for i in range(TILES):
                constants[0:1, rows_of(i)] = diagonal_row(inverse, i * T, i * T)
        else:
            constants[0:1, :] = jnp.zeros((1, B), F32)
        loads[2].wait()
        if is_leaf:
            step[...] = step_inverse[...].astype(F32) + lax.dot_general(
                first[...], lower[...], (((0,), (0,)), ((), ())), preferred_element_type=F32
            )
        else:
            step[...] = step_inverse[...].astype(F32)
        for i in range(TILES):
            constants[1:2, rows_of(i)] = diagonal_row(step, i * T, i * T)
        loads[3].wait()
        factors[:, B:] = mm(factors[:, :B], second[...]).astype(BF)
        last = mm(step[...].astype(BF), second[...])
        extra = jnp.sum(second[...].astype(F32) * last, axis=0, keepdims=True) + step_diagonal[...]
        constants[2:3, :] = extra
        constants[3:4, :] = jnp.full((1, B), float(is_leaf), F32)
        constants[4:8, :] = jnp.zeros((4, B), F32)


def prepare(is_leaf, active, coupler, step_diagonal, inverse, step_inverse, links, factors, constants):
    far = [pltpu.with_memory_space_constraint(a, pltpu.HBM) for a in (inverse, step_inverse, links)]
    block = pltpu.VMEM((B, B), BF)
    return pl.pallas_call(
        functools.partial(prepare_kernel, is_leaf),
        out_shape=(pltpu.VMEM((B, 2 * B), BF), pltpu.VMEM((8, B), F32)),
        in_specs=[SMEM, VMEM, VMEM, HBM, HBM, HBM, VMEM, VMEM],
        out_specs=(VMEM, VMEM),
        input_output_aliases={6: 0, 7: 1},
        scratch_shapes=[block, block, block, block, block, pltpu.VMEM((B, B), F32), pltpu.SemaphoreType.DMA((4,))],
        compiler_params=params(),
        cost_estimate=cost(5),
    )(active, coupler, step_diagonal, *far, factors, constants)


HEAD = 16
GATHERED = 4
ALL_ROWS = 8 << GATHERED


def halved(packed, i):
    row = packed[:, strip(i)]
    diagonal = row[:, :T] * BF(0.5)
    return diagonal if i == TILES - 1 else jnp.concatenate([diagonal, row[:, T:]], axis=1)


def block_forms(left, right):
    count = right.shape[0]
    high = left.astype(BF)
    low = (left - high.astype(F32)).astype(BF)
    gram = times_transposed(high, right) + times_transposed(low, right)
    rows = lax.broadcasted_iota(jnp.int32, (count, count), 0)
    columns = lax.broadcasted_iota(jnp.int32, (count, count), 1)
    gram = jnp.where(rows // 4 == columns // 4, gram, 0.0)
    folded = jnp.sum(gram.reshape(count // 8, 8, count), axis=0)
    folded = jnp.concatenate([folded[:4] + folded[4:], jnp.zeros((4, count), F32)], axis=0)
    if count < T:
        folded = jnp.concatenate([folded, jnp.zeros((8, T - count), F32)], axis=1)
    shift = T // 2
    while shift >= 4:
        folded = folded + pltpu.roll(folded, shift, 1)
        shift //= 2
    lanes = lax.broadcasted_iota(jnp.int32, (8, T), 1)
    return jnp.where(lanes < 4, folded, 0.0)


def packed_forms(rows, packed):
    parts = [mm(rows[:, rows_of(i)], halved(packed, i)) for i in range(TILES)]
    columns = []
    for i in range(TILES):
        column = parts[0][:, rows_of(i)]
        for k in range(1, i + 1):
            column = column + parts[k][:, (i - k) * T : (i - k + 1) * T]
        columns.append(column)
    form = block_forms(jnp.concatenate(columns, axis=1), rows)
    square = jnp.concatenate([form, jnp.zeros((T - 8, T), F32)], axis=0)
    return form + square.T[:8]


def write_constants(message, value):
    high = value.astype(BF).astype(F32)
    head = jnp.concatenate([high, value - high, jnp.zeros((8, T), F32)], axis=0)
    message[0:HEAD, 0:T] = head.astype(BF)


def constants_of(message):
    head = message[0:HEAD, 0:T].astype(F32)
    return jnp.concatenate([head[0:4] + head[4:8], jnp.zeros((4, T), F32)], axis=0)


def own_message_kernel(arrows, links_far, step_far, live_any, message, steps, link, step_inverse, live, sems):
    fetch(sems, (links_far.at[0, 0], link), (step_far, step_inverse), (live_any, live))
    steps[...] = jnp.full((8, T), live[0], jnp.int32).astype(F32)
    a0 = arrows[0, 0]
    a1 = arrows[0, 1]
    through = times_transposed(a1, link[...])
    own = jnp.concatenate([a0.astype(F32), through, jnp.zeros((8, B), F32)], axis=0)
    message[HEAD:, :] = own.astype(BF)
    zeros = jnp.zeros((4, B), BF)
    padded = jnp.concatenate([a1, zeros, zeros, zeros], axis=0)
    write_constants(message, block_forms(mm(padded, step_inverse[...]), padded)[:4])


def own_message(arrows, links, step_inverse, lengths):
    return pl.pallas_call(
        own_message_kernel,
        out_shape=(jax.ShapeDtypeStruct((HEAD + 16, B), BF), pltpu.VMEM((8, T), F32)),
        in_specs=[VMEM, HBM, HBM, ANY],
        out_specs=(VMEM, VMEM),
        scratch_shapes=[
            pltpu.VMEM((B, B), BF), pltpu.VMEM((B, B), BF), pltpu.SMEM((1,), jnp.int32),
            pltpu.SemaphoreType.DMA((3,)),
        ],
        compiler_params=params(),
        cost_estimate=cost(0.001),
    )(arrows, *[pltpu.with_memory_space_constraint(a, pltpu.HBM) for a in (links, step_inverse)], lengths)


def first_eight(message):
    return message[HEAD:, :].astype(F32)[:8]


HALF = ALL_ROWS // 2


def chip_rows_kernel(own, other, coupler, rows):
    rows[...] = jnp.zeros((HALF, B), BF)
    through = times_transposed(own[HEAD:, :], coupler[...])
    rows[0:16, :] = jnp.concatenate([first_eight(other), through[:8]], axis=0).astype(BF)


def chip_rows(own, other, coupler):
    return pl.pallas_call(
        chip_rows_kernel,
        out_shape=pltpu.VMEM((HALF, B), BF),
        in_specs=[VMEM] * 3,
        out_specs=VMEM,
        compiler_params=params(),
        cost_estimate=cost(0.2),
    )(own, other, coupler)


def chip_constants_kernel(own, other, inverse_far, sums, inverse, sems):
    fetch(sems, (inverse_far, inverse))
    mine = own[HEAD:, :]
    sums[...] = constants_of(own) + constants_of(other) + block_forms(mm(mine, inverse[...]), mine)


def chip_constants(own, other, inverse):
    return pl.pallas_call(
        chip_constants_kernel,
        out_shape=jax.ShapeDtypeStruct((8, T), F32),
        in_specs=[VMEM, VMEM, HBM],
        out_specs=VMEM,
        scratch_shapes=[pltpu.VMEM((B, B), BF), pltpu.SemaphoreType.DMA((1,))],
        compiler_params=params(),
        cost_estimate=cost(0.2),
    )(own, other, pltpu.with_memory_space_constraint(inverse, pltpu.HBM))


def up_kernel(stage, flags, coupler_any, incoming_any, _, rows, message, coupler, sems):
    if stage > 1:

        @pl.when(flags[0] == 1)
        def _():
            count = 8 << (stage - 1)
            fetch(sems, (incoming_any, rows.at[pl.ds(count, count)]))

    @pl.when(flags[1] == 1)
    def _():
        fetch(sems, (coupler_any, coupler))
        message[...] = times_transposed(rows[0 : 8 << stage, :], coupler[...]).astype(BF)


def up(stage, flags, coupler, incoming, rows):
    return pl.pallas_call(
        functools.partial(up_kernel, stage),
        out_shape=(pltpu.VMEM((HALF, B), BF), pltpu.VMEM((8 << stage, B), BF)),
        in_specs=[SMEM, ANY, ANY, VMEM],
        out_specs=(VMEM,) * 2,
        input_output_aliases={3: 0},
        scratch_shapes=[pltpu.VMEM((B, B), BF), pltpu.SemaphoreType.DMA((1,))],
        compiler_params=params(),
        cost_estimate=cost(0.3),
    )(flags, coupler, incoming, rows)


def finish_kernel(rows, out):
    out[...] = rows[...]


def finish(rows):
    return pl.pallas_call(
        finish_kernel,
        out_shape=jax.ShapeDtypeStruct(rows.shape, BF),
        in_specs=[VMEM],
        out_specs=VMEM,
        compiler_params=params(),
        cost_estimate=cost(0.1),
    )(rows)


def absorb_kernel(
    scale, flags, block_any, state_any, incoming_any, rows, sums, tips, block, gathered, sems
):
    gathered[0:HALF, :] = rows[...]

    @pl.when(flags[0] == 1)
    def _():
        fetch(sems, (state_any, block), (incoming_any, gathered.at[pl.ds(HALF, HALF)]))

    @pl.when(flags[0] != 1)
    def _():
        gathered[HALF:, :] = jnp.zeros((HALF, B), BF)
        fetch(sems, (block_any, block))

    value = sums[...] + packed_forms(gathered[...], block)
    row = value[0:1]
    for j in range(1, 4):
        row = row + pltpu.roll(value[j : j + 1], 4 * j, 1)
    tips[...] = jnp.broadcast_to((row * scale)[None], tips.shape)


def absorb(scale, flags, block_zero, state_zero, incoming, rows, sums, copies):
    return pl.pallas_call(
        functools.partial(absorb_kernel, scale),
        out_shape=jax.ShapeDtypeStruct((copies, 1, T), F32),
        in_specs=[SMEM, ANY, ANY, ANY, VMEM, VMEM],
        out_specs=VMEM,
        scratch_shapes=[
            pltpu.VMEM((T, PACKED), BF), pltpu.VMEM((ALL_ROWS, B), BF), pltpu.SemaphoreType.DMA((2,)),
        ],
        compiler_params=params(),
        cost_estimate=cost(0.5),
    )(flags, block_zero, state_zero, incoming, rows, sums)


def tail_kernel(
    received, state, coupler, factors, constants, steps, tip, tip_received, variances, tip_out
):
    leaf = constants[3:4, 0:1] == 1.0
    totals = [jnp.zeros((8, B), F32) for _ in range(3)]
    for i in range(TILES):
        row = jnp.where(leaf, received[:, strip(i)].astype(F32), state[:, strip(i)].astype(F32))
        halves = [row[:, :T] * 0.5, row[:, T:]]
        upper = jnp.concatenate(halves[: 2 if i < TILES - 1 else 1], axis=1).astype(BF)
        for k, (block, start) in enumerate(((coupler, 0), (factors, 0), (factors, B))):
            product = mm(upper, block[i * T :, start : start + B])
            terms = product * block[rows_of(i), start : start + B].astype(F32)
            totals[k] = totals[k] + jnp.sum(terms.reshape(T // 8, 8, B), axis=0)
    values = [
        constants[k : k + 1, :] + 2.0 * jnp.sum(total, axis=0, keepdims=True)
        for k, total in enumerate(totals)
    ]
    for i in range(TILES):
        own = diagonal_row(state, 0, STARTS[i])
        variances[0, :, rows_of(i)] = jnp.where(leaf, values[0][:, rows_of(i)], own)
    variances[1] = values[1]
    variances[2] = jnp.where(steps[0:1, 0:1] == 2.0, values[2], 0.0)
    row = jnp.where(leaf, tip[...], tip_received[...])
    for j in range(4):
        turned = row if j == 0 else pltpu.roll(row, T - 4 * j, 1)
        tip_out[j : j + 1, :] = turned[:, 0:4]


def tail(received, state, coupler, factors, constants, steps, tip, tip_received):
    return pl.pallas_call(
        tail_kernel,
        out_shape=(
            jax.ShapeDtypeStruct((3, 1, B), F32),
            jax.ShapeDtypeStruct((4, 4), F32),
        ),
        in_specs=[VMEM] * 8,
        out_specs=(VMEM, VMEM),
        compiler_params=params(),
        cost_estimate=cost(3),
    )(received, state, coupler, factors, constants, steps, tip, tip_received)


def blank_kernel(out):
    pass


def blank(shape, dtype, kind=jax.ShapeDtypeStruct):
    return pl.pallas_call(
        blank_kernel,
        out_shape=kind(shape, dtype),
        out_specs=VMEM if kind is pltpu.VMEM else ANY,
        compiler_params=params(),
        cost_estimate=cost(0.001),
    )()


def swap_pairs(devices, bit):
    return [(i, i ^ bit) for i in range(devices)]


def chip_cycles(devices, height):
    target = {i: i ^ 1 for i in range(devices)}
    for child in range(1 << height, devices, 2 << height):
        parent = child - (1 << height)
        target[parent] = child
        target[child] = child + 1
        target[child + 1] = parent + 1
        target[parent + 1] = parent
    return sorted(target.items())


def neighbour_cycles(devices, height, offset):
    target = {i: i ^ 1 for i in range(devices)}
    for child in range(1 << height, devices, 2 << height):
        for core in range(2):
            first, second = child - (1 << height) + core, child + core
            target[first] = second
            target[second] = second + offset
            target[second + offset] = first + offset
            target[first + offset] = first
    return sorted(target.items())


def children(devices, source, target):
    return [(row + 2 * source, row + 2 * target) for row in range(0, devices, 8)]


def row_cycles(devices, cycle):
    return [
        (row + 2 * cycle[k - 1] + core, row + 2 * cycle[k] + core)
        for row in range(0, devices, 8)
        for k in range(4)
        for core in range(2)
    ]


def summing_order(devices):
    def place(chip):
        layer = chip % 64 // 8
        early = layer if layer < 4 else 11 - layer
        if chip % (1 << GATHERED) == 0:
            return (1, early, chip // 64)
        return (0, -early, -(chip // 64), -(chip % 8))

    return sorted(range(0, devices, 2), key=place)


def after(arrays, *others):
    return lax.optimization_barrier((arrays, others))[0]


def integers(*values):
    return jnp.stack([jnp.asarray(value, jnp.int32) for value in values])


def shards(boundary_inverse, coupling, step_inverse, step_diagonal, links, arrows, lengths):
    blocks = lax.axis_size("tm")
    me = lax.axis_index("tm")
    chip = me - me % 2
    on_core_one = me % 2 == 1
    inverse = boundary_inverse[0]
    step_inv = step_inverse[0]
    swap = swap_pairs(blocks, 1)
    absorbs = chip % (1 << GATHERED) == 0

    def send(array, pairs):
        return lax.ppermute(array, "tm", pairs)

    def descend(height, parent, state):
        active = integers(me % (2 << height) == 1 << height)
        return level(active, parent, coupler, turned, state)

    def helper(height):
        return 6 if height % 2 else 2

    def takes_part(height):
        place = me % (1 << height)
        return (place == 0) | (place == helper(height))

    def is_sender(stage):
        return chip % (2 << stage) == 1 << stage

    def is_receiver(stage):
        return chip % (2 << stage) == 0

    state = pack(inverse)

    parent = send(state, chip_cycles(blocks, 7))
    given = after((arrows, links, step_inv), state)
    mine, steps = own_message(*given, lengths)
    factors = blank((B, 2 * B), BF, pltpu.VMEM)
    constants = blank((8, B), F32, pltpu.VMEM)
    coupler, turned = open_coupler(after(coupling[0], mine))
    coupler_zero = send(coupling[0], swap)
    message_zero = send(mine, swap)
    block_zero = parent
    parent, coupler_zero, message_zero = lax.optimization_barrier((parent, coupler_zero, message_zero))
    state = descend(7, parent, state)

    def get_ready(is_leaf, active, factors, constants, *others):
        given = after((step_diagonal, inverse, step_inv, links), *others)
        return list(prepare(is_leaf, integers(active), coupler, *given, factors, constants))

    def tree_top(state, factors, constants):
        factors, constants = get_ready(False, chip % 64 != 0, factors, constants)
        for height in (6, 5, 4):
            state = lax.cond(
                takes_part(height),
                lambda s, h=height: descend(h, send(s, neighbour_cycles(blocks, h, helper(h))), s),
                lambda s: s,
                state,
            )
        return [state, blank((HALF, B), BF), blank((HALF, B), BF), blank((8, T), F32), factors, constants]

    def gather_rows(state, factors, constants):
        rows = chip_rows(mine, message_zero, coupler)
        message = message_zero
        sums = None
        for stage in range(1, GATHERED):
            flags = integers(is_receiver(stage - 1), is_sender(stage))
            rows, message = up(stage, flags, coupler_zero, message, rows)
            message = send(message, swap_pairs(blocks, 1 << stage))
            if sums is None:
                sums = chip_constants(mine, message_zero, after(inverse, rows))
                message, sums = lax.optimization_barrier((message, sums))
        rows = finish(rows)
        return [state, rows, message, sums, *get_ready(True, 1, factors, constants, message)]

    state, rows, message, sums, factors, constants = lax.cond(
        on_core_one, gather_rows, tree_top, state, factors, constants
    )

    def middle(state, factors, constants):
        parent = send(copied(state), chip_cycles(blocks, 3))
        state_zero = send(state, swap)
        factors, constants = get_ready(False, me % 64 == 0, factors, constants, state)
        parent, state_zero, factors, constants = lax.optimization_barrier(
            (parent, state_zero, factors, constants)
        )
        return [descend(3, parent, state), state_zero, factors, constants]

    state, state_zero, factors, constants = lax.cond(
        chip % 8 == 0, middle, lambda s, f, c: [s, blank((T, PACKED), BF), f, c], state, factors, constants
    )

    def sum_tips(state):
        tips = absorb(
            1.0 / (2 * blocks), integers(absorbs), block_zero, state_zero, message, rows, sums, blocks // 2
        )
        every = lax.all_to_all(
            tips, "tm", 0, 0,
            axis_index_groups=[[chip + core for chip in summing_order(blocks)] for core in range(2)],
        )
        return [state, jnp.sum(every, axis=0), finish(state_zero)]

    def tree_bottom(state):
        place = me % 8
        to_third = send(copied(state), row_cycles(blocks, (0, 2, 3, 1)))
        to_second = send(state, children(blocks, 0, 1))
        to_third, before = lax.optimization_barrier((to_third, state))
        state = level(integers(place == 4), to_third, coupler, turned, before)
        to_fourth = send(state, children(blocks, 2, 3))
        state = level(integers(place == 2), after(to_second, state), coupler, turned, state)
        state = level(integers(place == 6), to_fourth, coupler, turned, state)
        return [state, blank((1, T), F32), blank((T, PACKED), BF)]

    state, tip, held = lax.cond(on_core_one, sum_tips, tree_bottom, state)
    parent = lax.cond(absorbs, lambda s, z: z, lambda s, z: send(s, swap), state, held)
    tip_received = send(tip, swap)
    variances, total = tail(parent, state, coupler, factors, constants, steps, tip, tip_received)
    return jnp.transpose(variances, (1, 0, 2)), total


def solution(mesh):
    in_specs = (
        P("tm", None, None),
        P("tm", None, None),
        P("tm", None, None),
        P("tm", None),
        P("tm", None, None, None),
        P("tm", None, None, None),
        P("tm"),
    )
    out_specs = (P("tm", None, None), P())
    return jax.shard_map(shards, mesh=mesh, in_specs=in_specs, out_specs=out_specs, check_vma=False)
```
